512 devices in a mesh: seq: 8 (over z_lo, core), vocab: 64 (over y, x, z_hi).
Axes of the slice: x: 4, y: 8, z: 8 (z_hi: 2, z_lo: 4; z = z_hi * 4 + z_lo), core: 2. Of those that a mesh axis runs over, the one named last changes fastest.
Arguments:
- posteriors: bfloat16 [32768, 16384], P(('seq', 'vocab')), may hold values from 0.2 to 2300, as said below
- token_block: int32 [32768, 1], P(('seq', 'vocab')), may hold values from 0 to 63; in each aligned block of 64 rows (0 to 63, 64 to 127, ...) at most 2 rows name the same one
- token_offset: int32 [32768], P(('seq', 'vocab')), may hold values from 0 to 255
- lengths: int32 [8], replicated, may hold values from 2048 to 4096, as said below
- smoothing: float32 [16384], P('seq'), may hold values from 4 to 40
Outputs:
- emission: float32 [16384, 16384], P('seq', 'vocab')
The draws below stay inside these ranges and needn't reach their ends.
Inputs may be any that keep to these rules, and one draw needn't show every extreme that they name: `posteriors`: all entries are positive. `lengths`: some group is live over all its positions.
All inputs are finite; a program needn't handle non-finite values.
Results may differ from the reference program's by a relative error of at most 0.0003.
Values may be sent and summed in bfloat16 or wider, within the bound.
No kernel may reach another device: no remote copies, remote signals or barrier semaphores. Data moves between devices by JAX's collectives and lax.ppermute only.
A program may use at most 64 MiB of HBM per device.

```python
import math
import jax
import jax.numpy as jnp
import numpy as np
from jax import lax

STATES = 16384
VOCAB = 16384
TOK_DEV = 64
GROUPS = 8
VLOC = 256
CAP = 2
GP = 4096
POSITIONS = 32768
N_VOCAB = 64


def draw_posteriors(key, part):
    key = jax.random.fold_in(key, 11)
    key_rows, key_cols, key_cells = jax.random.split(key, 3)
    row_scale = jnp.exp(jax.random.uniform(key_rows, (POSITIONS, 1), jnp.float32) * math.log(10.0))
    col_scale = jnp.exp(jax.random.uniform(key_cols, (1, STATES), jnp.float32) * math.log(10.0))
    ramp_frac = (jnp.arange(POSITIONS, dtype=jnp.float32) / POSITIONS)[:, None]
    ramp = jnp.exp(ramp_frac * math.log(3.0))
    cells = jnp.exp(jax.random.uniform(key_cells, (POSITIONS, STATES), jnp.float32, -0.7, 0.7))
    return (row_scale * col_scale * ramp * cells).astype(jnp.bfloat16)


def draw_lengths(key, part):
    key = jax.random.fold_in(key, 5)
    key_base, key_full = jax.random.split(key, 2)
    base_lengths = jax.random.randint(key_base, (GROUPS,), GP // 2, GP + 1, dtype=jnp.int32)
    full_group = jax.random.randint(key_full, (), 0, GROUPS, dtype=jnp.int32)
    return jnp.where(jnp.arange(GROUPS, dtype=jnp.int32) == full_group, GP, base_lengths).astype(jnp.int32)


def touch_ends(drawn, key, low, high):
    longest = drawn.shape.index(max(drawn.shape))
    spots = []
    for shift in (0, 1):
        where = [jax.random.randint(jax.random.fold_in(key, axis), (), 0, length) for axis, length in enumerate(drawn.shape)]
        where[longest] = (where[longest] + shift) % drawn.shape[longest]
        spots.append(tuple(where))
    return drawn.at[spots[0]].set(low).at[spots[1]].set(high)


def levels(stream_key, extent, cuts, smallest, top_value):
    loudness, own = 1.0, jax.random.fold_in(stream_key, 6)
    for axis_at, parts in cuts:
        heights = jnp.exp(jax.random.uniform(jax.random.fold_in(own, axis_at), (parts,), jnp.float32, smallest / len(cuts), top_value / len(cuts)))
        loudness = loudness * jnp.repeat(heights, extent[axis_at] // parts).reshape([-1 if axis == axis_at else 1 for axis in range(len(extent))])
    return loudness


def shared_out(stream_key, own, number, rows, count, top, limit, lean):
    ranking = jax.random.permutation(stream_key, count)
    heavy_load, ordinary = portions_of(count, rows * top, limit, lean, True), portions_of(count, rows * top, limit, lean, False)
    places = jnp.arange(count)

    def named(sizes, offset_by):
        used = int((sizes > 0).sum())
        fixed = max(1, used // 4)
        passed = fixed + (places - fixed + offset_by * (used - fixed)) % max(1, count - fixed)
        return jnp.zeros((count,), jnp.int32).at[ranking[jnp.where(places < fixed, places, passed)]].set(jnp.asarray(sizes, jnp.int32))

    sizes = jnp.where(number % 4 == 0, named(heavy_load, number // 4), named(ordinary, number - number // 4 - 1))
    mixed = jax.random.permutation(jax.random.fold_in(own, 3), count)
    donor, receiver = mixed[0:count // 2 * 2:2], mixed[1:count // 2 * 2:2]
    room = jnp.minimum(sizes[donor] - 1, limit - sizes[receiver]) // 2
    room = jnp.where((donor == ranking[0]) | (receiver == ranking[0]) | (sizes[receiver] == 0), 0, jnp.maximum(room, 0))
    passed = jax.random.randint(jax.random.fold_in(own, 4), (count // 2,), 0, 1 << 20) % (room + 1)
    sizes = sizes.at[donor].add(-passed).at[receiver].add(passed)
    members = jnp.searchsorted(jnp.cumsum(sizes), jnp.arange(rows * top), side="right").astype(jnp.int32)
    table = members.reshape(top, rows).T
    table = table[jax.random.permutation(jax.random.fold_in(own, 1), rows)]
    offset_by = jax.random.randint(jax.random.fold_in(own, 2), (rows, 1), 0, top)
    return jnp.take_along_axis(table, (jnp.arange(top)[None, :] + offset_by) % top, axis=1)


def portions_of(count, total, most, skew, full):
    portions = [(1 << 20) // math.isqrt(standing ** skew) + 1 for standing in range(1, count + 1)]
    largest = most if full else min(most, max(-(-total // count), total * portions[0] // sum(portions)))
    least = 1 if total - largest >= count - 1 else 0
    counts, spare = [largest] + [least] * (count - 1), total - largest - least * (count - 1)
    while spare > 0:
        candidates = [i for i in range(1, count) if counts[i] < largest] or [i for i in range(1, count) if counts[i] < most]
        mass, remaining = sum([portions[i] for i in candidates]), spare
        for i in candidates:
            addition = min(most - counts[i], max(1, remaining * portions[i] // mass), spare)
            counts[i] = counts[i] + addition
            spare = spare - addition
    return np.array(counts)


def setup_inputs(seed: int = 0) -> dict:
    splits = jax.random.split(jax.random.key(seed), 6)
    posteriors = draw_posteriors(jax.random.fold_in(splits[5], 71), 0)
    token_block_keys = jax.random.split(jax.random.fold_in(splits[1], 1), POSITIONS // TOK_DEV)
    token_block_turns = jax.random.permutation(jax.random.fold_in(splits[1], 3), POSITIONS // TOK_DEV)
    token_block = jax.vmap(lambda own, number: shared_out(jax.random.fold_in(splits[1], 2), own, number, TOK_DEV, N_VOCAB, 1, CAP, 1))(token_block_keys, token_block_turns).reshape((POSITIONS, 1))
    token_offset = touch_ends(jax.random.randint(splits[2], (POSITIONS,), 0, VLOC), jax.random.fold_in(splits[2], 1), 0, VLOC - 1).astype(jnp.int32)
    lengths = draw_lengths(jax.random.fold_in(splits[5], 71), 0)
    smoothing = jnp.clip(jnp.exp(math.log(40.0) - 2.3025851 * jax.random.uniform(splits[4], (STATES,), jnp.float32) ** levels(splits[4], (STATES,), ((0, 8),), -0.2, 0.2)), 4.0, 40.0)
    return {"posteriors": posteriors, "token_block": token_block, "token_offset": token_offset, "lengths": lengths, "smoothing": smoothing}


def reference(posteriors, token_block, token_offset, lengths, smoothing):
    token_ids = token_block[:, 0] * VLOC + token_offset
    position = jnp.arange(POSITIONS, dtype=jnp.int32)
    group_index = position // GP
    keep_mask = ((position % GP) < lengths[group_index]).astype(jnp.float32)

    def add_group(running, inputs):
        rows, group_ids, weights = inputs
        terms = rows.astype(jnp.float32) * weights[:, None]
        return running + jax.ops.segment_sum(terms, group_ids, num_segments=VOCAB), None

    running = jnp.zeros((VOCAB, STATES), jnp.float32)
    running, unused = lax.scan(add_group, running, (posteriors.reshape(GROUPS, GP, STATES), token_ids.reshape(GROUPS, GP), keep_mask.reshape(GROUPS, GP)))
    totals = jnp.sum(running, axis=0)
    pseudo = smoothing * (POSITIONS / VOCAB)
    scaled = VOCAB * (running + pseudo[None, :]) / (totals[None, :] + VOCAB * pseudo[None, :])
    return scaled.T
```

```python
import jax
import jax.numpy as jnp
from jax import lax
from jax.sharding import Mesh, PartitionSpec as P

VOCAB = 16384
SEQ = ("zlo", "core")
VOC = ("y", "x", "zhi")


def shards(posteriors, token_block, token_offset, lengths, smoothing):
    rows, states = posteriors.shape
    vocab_devs = lax.axis_size(VOC)
    seq_devs = lax.axis_size(SEQ)
    capacity = 2
    width = VOCAB // vocab_devs
    state_rows = states // seq_devs
    ratio = rows * vocab_devs * seq_devs / VOCAB
    me_v = lax.axis_index(VOC)
    me_s = lax.axis_index(SEQ)

    position = me_v * rows + jnp.arange(rows, dtype=jnp.int32)
    live = position < lengths[me_s]
    block = token_block[:, 0]
    same = (block[:, None] == block[None, :]) & live[None, :]
    row_ids = jnp.arange(rows, dtype=jnp.int32)
    rank = jnp.sum((same & (row_ids[None, :] < row_ids[:, None])).astype(jnp.int32), axis=1)
    slot = jnp.where(live, block * capacity + rank, -1)
    pick = (jnp.arange(vocab_devs * capacity, dtype=jnp.int32)[:, None] == slot[None, :]).astype(
        jnp.bfloat16
    )
    cube = posteriors.reshape(rows, seq_devs, state_rows)
    buckets = jnp.einsum("kr,rsn->skn", pick, cube, preferred_element_type=jnp.float32)
    buckets = buckets.astype(jnp.bfloat16).reshape(seq_devs * vocab_devs, capacity, state_rows)
    got = lax.all_to_all(buckets, SEQ + VOC, split_axis=0, concat_axis=0, tiled=True)

    part = jnp.dot(
        live.astype(jnp.bfloat16)[None, :], posteriors, preferred_element_type=jnp.float32
    )[0]
    tags = jnp.where(live, block * width + token_offset, -1).astype(jnp.float32)

    def place(values, axis):
        size = lax.axis_size(axis)
        hit = jnp.arange(size) == lax.axis_index(axis)
        return jnp.where(hit[:, None], values[None, :], 0.0).reshape(-1)

    joined = lax.psum(jnp.concatenate([part, place(tags, SEQ)]), SEQ)
    totals = lax.dynamic_slice(joined, (me_s * state_rows,), (state_rows,))
    tags = joined[states:]
    for axis in ("zhi", "x", "y"):
        joined = lax.psum(jnp.concatenate([totals, place(tags, axis)]), axis)
        totals, tags = joined[:state_rows], joined[state_rows:]
    tags = tags.astype(jnp.int32).reshape(vocab_devs, seq_devs, rows)
    tags = tags.transpose(1, 0, 2).reshape(vocab_devs * seq_devs, rows)
    big = rows * width
    keys = jnp.where(
        (tags >= me_v * width) & (tags < (me_v + 1) * width),
        row_ids[None, :] * width + tags - me_v * width,
        big,
    )
    first = jnp.min(keys, axis=1)
    second = jnp.min(jnp.where(keys > first[:, None], keys, big), axis=1)
    both = jnp.stack([first, second], axis=1)
    offset = jnp.where(both < big, both % width, -1).reshape(-1)

    one_hot = (offset[None, :] == jnp.arange(width, dtype=jnp.int32)[:, None]).astype(jnp.bfloat16)
    counts = jnp.dot(one_hot, got.reshape(-1, state_rows), preferred_element_type=jnp.float32)
    pseudo = smoothing * ratio
    emission = VOCAB * (counts + pseudo[None, :]) / (totals[None, :] + VOCAB * pseudo[None, :])
    return emission.T


def solution(mesh):
    fine = Mesh(mesh.devices.reshape(4, 2, 8, 4, 2), SEQ + VOC)
    placed = (P(SEQ + VOC, None), P(SEQ + VOC, None), P(SEQ + VOC), P(), P(SEQ))
    return jax.shard_map(
        shards, mesh=fine, in_specs=placed, out_specs=P(SEQ, VOC), check_vma=False
    )
```

```python
import jax
import jax.numpy as jnp
from jax import lax
from jax.sharding import Mesh, PartitionSpec as P

VOCAB = 16384
SEQ = ("z1", "z0", "core")
VOC = ("y2", "y1", "y0", "x1", "x0", "zhi")
LANES = 128


def swap(values, axis):
    return lax.ppermute(values, axis, [(0, 1), (1, 0)])


def small_exchange(part, table):
    seq_devs = lax.axis_size(SEQ)
    vocab_devs = table.shape[0]
    state_rows = part.shape[0] // seq_devs
    tot_rows = state_rows // LANES
    tags = jnp.broadcast_to(table[:, None, :], (vocab_devs, seq_devs, 2)).reshape(-1, LANES)
    tag_rows = tags.shape[0]
    index = lax.broadcasted_iota(jnp.int32, tags.shape, 0) * LANES + lax.broadcasted_iota(
        jnp.int32, tags.shape, 1
    )
    q = (index // 2) % seq_devs
    r = index // (2 * seq_devs)
    cur = part.reshape(seq_devs, tot_rows, LANES)
    for at, axis in reversed(list(enumerate(SEQ))):
        bit = lax.axis_index(axis)
        low = cur.reshape(-1, 2, tot_rows, LANES)
        keep = jnp.where(bit == 0, low[:, 0], low[:, 1])
        send = jnp.where(bit == 0, low[:, 1], low[:, 0])
        n = send.shape[0] * tot_rows
        got = swap(jnp.concatenate([send.reshape(n, LANES), tags]), axis)
        cur = keep + got[:n].reshape(keep.shape)
        side = (q >> (len(SEQ) - 1 - at)) & 1
        tags = jnp.where(side == 1, got[n:], tags)
    both = jnp.concatenate([cur.reshape(tot_rows, LANES), tags])
    pos = lax.broadcasted_iota(jnp.int32, both.shape, 0) * LANES + lax.broadcasted_iota(
        jnp.int32, both.shape, 1
    )
    rel = (pos - state_rows) // (2 * seq_devs)
    for at, axis in reversed(list(enumerate(VOC))):
        got = swap(both, axis)
        side = (rel >> (len(VOC) - 1 - at)) & 1
        both = jnp.where(pos < state_rows, both + got, jnp.where(side == 1, got, both))
    totals = both[:tot_rows].reshape(state_rows)
    tags = both[tot_rows:].reshape(vocab_devs, seq_devs * 2)
    return totals, tags


def absolute(tags, me_s, me_v):
    vocab_devs, width = tags.shape
    v = jnp.arange(vocab_devs)
    c = jnp.arange(width)
    left = ((v[:, None] ^ v[None, :]) == me_v).astype(jnp.bfloat16)
    right = ((c[:, None] ^ c[None, :]) == 2 * me_s).astype(jnp.bfloat16)
    tags = jnp.dot(left, tags.astype(jnp.bfloat16), preferred_element_type=jnp.float32)
    tags = jnp.dot(tags.astype(jnp.bfloat16), right, preferred_element_type=jnp.float32)
    tags = tags.reshape(vocab_devs, width // 2, 2)
    return tags.transpose(1, 0, 2).reshape(-1)


def shards(posteriors, token_block, token_offset, lengths, smoothing):
    rows, states = posteriors.shape
    vocab_devs = lax.axis_size(VOC)
    seq_devs = lax.axis_size(SEQ)
    capacity = 2
    width = VOCAB // vocab_devs
    state_rows = states // seq_devs
    ratio = rows * vocab_devs * seq_devs / VOCAB
    me_v = lax.axis_index(VOC)
    me_s = lax.axis_index(SEQ)

    position = me_v * rows + jnp.arange(rows, dtype=jnp.int32)
    live = position < lengths[me_s]
    block = token_block[:, 0]
    same = (block[:, None] == block[None, :]) & live[None, :]
    row_ids = jnp.arange(rows, dtype=jnp.int32)
    rank = jnp.sum((same & (row_ids[None, :] < row_ids[:, None])).astype(jnp.int32), axis=1)
    slot = jnp.where(live, block * capacity + rank, -1)
    slots = jnp.arange(vocab_devs * capacity, dtype=jnp.int32)
    pick = (slots[:, None] == slot[None, :]).astype(jnp.bfloat16)
    cube = posteriors.reshape(rows, seq_devs, state_rows)
    buckets = jnp.einsum("kr,rsn->skn", pick, cube, preferred_element_type=jnp.float32)
    buckets = buckets.astype(jnp.bfloat16).reshape(seq_devs * vocab_devs, capacity, state_rows)
    got = lax.all_to_all(buckets, SEQ + VOC, split_axis=0, concat_axis=0, tiled=True)

    part = jnp.dot(
        live.astype(jnp.bfloat16)[None, :], posteriors, preferred_element_type=jnp.float32
    )[0]
    rel_hit = (slots ^ (2 * me_v))[:, None] == slot[None, :]
    table = jnp.sum(jnp.where(rel_hit, token_offset[None, :] + 1, 0), axis=1) - 1
    table = table.astype(jnp.float32).reshape(vocab_devs, capacity)
    totals, tags = small_exchange(part, table)
    offset = absolute(tags, me_s, me_v)

    one_hot = (
        offset[None, :] == jnp.arange(width, dtype=jnp.int32)[:, None].astype(jnp.float32)
    ).astype(jnp.bfloat16)
    counts = jnp.dot(one_hot, got.reshape(-1, state_rows), preferred_element_type=jnp.float32)
    pseudo = smoothing * ratio
    emission = VOCAB * (counts + pseudo[None, :]) / (totals[None, :] + VOCAB * pseudo[None, :])
    return emission.T


def solution(mesh):
    fine = Mesh(mesh.devices.reshape((2,) * (len(SEQ) + len(VOC))), SEQ + VOC)
    placed = (P(SEQ + VOC, None), P(SEQ + VOC, None), P(SEQ + VOC), P(), P(SEQ))
    return jax.shard_map(
        shards, mesh=fine, in_specs=placed, out_specs=P(SEQ, VOC), check_vma=False
    )
```

```python
import functools

import jax
import jax.numpy as jnp
from jax import lax
from jax.experimental import pallas as pl
from jax.experimental.pallas import tpu as pltpu
from jax.sharding import Mesh, PartitionSpec as P

VOCAB = 16384
SEQ = ("zlo", "core")
VOC = ("y", "x", "zhi")
TEAM = ("zlo", "core", "x")
LANES = 128
CAP = 2
HALF = 64
F32 = jnp.float32
BF16 = jnp.bfloat16
VMEM_LIMIT = 60 * 2**20


def live_rows(rows, lengths_ref):
    bound = lengths_ref[lax.axis_index(SEQ)] - lax.axis_index(VOC) * rows
    return lambda shape, dim: lax.broadcasted_iota(jnp.int32, shape, dim) < bound


def part_kernel(rows, seq_devs, slice_rows, lengths_ref, x_ref, o_ref, acc_ref):
    s = pl.program_id(0)
    shape = (seq_devs, rows)
    live = live_rows(rows, lengths_ref)(shape, 1)
    mine = lax.broadcasted_iota(jnp.int32, shape, 0) == s
    left = jnp.where(live & mine, 1.0, 0.0).astype(BF16)
    term = jnp.dot(left, x_ref[...], preferred_element_type=F32)

    @pl.when(s == 0)
    def _():
        acc_ref[...] = term

    @pl.when(s > 0)
    def _():
        acc_ref[...] += term

    @pl.when(s == seq_devs - 1)
    def _():
        for t in range(slice_rows // LANES):
            tile = acc_ref[:, t * LANES : (t + 1) * LANES]
            o_ref[2 * t] = tile
            o_ref[2 * t + 1] = pltpu.roll(tile, HALF, 1)


def bucket_kernel(rows, slots, lengths_ref, blk_ref, off_ref, x_ref, o_ref, tag_ref, pick_ref):
    slice_rows = x_ref.shape[1]

    @pl.when(pl.program_id(0) == 0)
    def _():
        shape = (slots, rows)
        live = live_rows(rows, lengths_ref)(shape, 1)
        k = lax.broadcasted_iota(jnp.int32, shape, 0)
        hit = live & (blk_ref[...] == k // CAP)
        before = lax.broadcasted_iota(jnp.int32, (rows, rows), 0) < lax.broadcasted_iota(
            jnp.int32, (rows, rows), 1
        )
        rank = jnp.dot(
            jnp.where(hit, 1.0, 0.0).astype(BF16),
            jnp.where(before, 1.0, 0.0).astype(BF16),
            preferred_element_type=F32,
        )
        pick = hit & (rank == (k % CAP).astype(F32))
        pick_ref[...] = jnp.where(pick, 1.0, 0.0).astype(BF16)
        value = jnp.where(pick, (off_ref[...] + 1).astype(F32), 0.0)
        tag = jnp.sum(value, axis=1, keepdims=True) - 1.0
        lane = lax.broadcasted_iota(jnp.int32, (slots, LANES), 1)
        tag_ref[...] = jnp.where(lane == HALF, tag, 0.0)

    y = jnp.dot(pick_ref[...], x_ref[...], preferred_element_type=F32).astype(BF16)
    o_ref[:, :, :slice_rows] = y.reshape(slots // CAP, CAP, slice_rows)
    o_ref[:, :, slice_rows:] = jnp.zeros((slots // CAP, CAP, LANES), BF16)


def carry_kernel(seq_devs, slots, sums_ref, tag_ref, send_ref, o_ref):
    del send_ref
    total = jnp.sum(sums_ref[...], axis=0)
    high = total.astype(BF16).astype(F32)
    low = total - high
    shape = (slots, LANES)
    odd = lax.broadcasted_iota(jnp.int32, shape, 0) % CAP == 1
    lane = lax.broadcasted_iota(jnp.int32, shape, 1)
    tag = tag_ref[...]
    n = slots // CAP
    for s in range(seq_devs):
        both = jnp.where(odd, low[s : s + 1], high[s : s + 1])
        carry = jnp.where(lane < HALF, both, tag).astype(BF16)
        o_ref[s * n : (s + 1) * n] = carry.reshape(n, CAP, LANES)


def final_kernel(dims, ratio, smooth_ref, data_ref, carry_ref, o_ref, hot_ref, tot_ref):
    seq_devs, y_devs, x_devs, h_devs = dims
    p = pl.program_id(0)
    kk = seq_devs * y_devs * x_devs * h_devs * CAP
    width = o_ref.shape[1]
    cols = data_ref.shape[2]
    tiles = cols // LANES

    @pl.when(p == 0)
    def _():
        carry = carry_ref[...].reshape(kk, LANES)
        sel = lax.broadcasted_iota(jnp.int32, (16, LANES), 1) == HALF
        off = lax.dot_general(
            jnp.where(sel, 1.0, 0.0).astype(BF16),
            carry,
            (((1,), (1,)), ((), ())),
            preferred_element_type=F32,
        )[0:1]
        v = lax.broadcasted_iota(jnp.int32, (width, kk), 0).astype(F32)
        hot_ref[...] = jnp.where(off == v, 1.0, 0.0).astype(BF16)
        n = tot_ref.shape[0]
        k = lax.broadcasted_iota(jnp.int32, (n, kk), 1)
        member = (k // (kk // seq_devs)) * x_devs + (k // (CAP * h_devs)) % x_devs
        t = lax.broadcasted_iota(jnp.int32, (n, kk), 0)
        even = jnp.where(member == 2 * t, 1.0, 0.0).astype(BF16)
        odd = jnp.where(member == 2 * t + 1, 1.0, 0.0).astype(BF16)
        even = jnp.dot(even, carry, preferred_element_type=F32)
        odd = jnp.dot(odd, carry, preferred_element_type=F32)
        lane = lax.broadcasted_iota(jnp.int32, (n, LANES), 1)
        tot_ref[...] = jnp.where(lane < HALF, even, pltpu.roll(odd, HALF, 1))

    counts = jnp.dot(hot_ref[...], data_ref[...].reshape(kk, cols), preferred_element_type=F32)
    for i in range(tiles):
        pseudo = smooth_ref[pl.ds(p * tiles + i, 1), :] * ratio
        scale = VOCAB / (tot_ref[pl.ds(p * tiles + i, 1), :] + VOCAB * pseudo)
        done = (counts[:, i * LANES : (i + 1) * LANES] + pseudo) * scale
        o_ref[i * LANES : (i + 1) * LANES, :] = done.T


def shards(posteriors, token_block, token_offset, lengths, smoothing):
    rows, states = posteriors.shape
    seq_devs = lax.axis_size(SEQ)
    vocab_devs = lax.axis_size(VOC)
    devs = seq_devs * vocab_devs
    team = lax.axis_size(TEAM)
    width = VOCAB // vocab_devs
    slice_rows = states // seq_devs
    slots = vocab_devs * CAP
    chunk = slice_rows + LANES
    ratio = rows * devs / VOCAB
    params = pltpu.CompilerParams(vmem_limit_bytes=VMEM_LIMIT)
    smem = pl.BlockSpec(memory_space=pltpu.SMEM)
    x_spec = pl.BlockSpec((rows, slice_rows), lambda s: (0, s))

    part = pl.pallas_call(
        functools.partial(part_kernel, rows, seq_devs, slice_rows),
        grid=(seq_devs,),
        in_specs=[smem, x_spec],
        out_specs=pl.BlockSpec((team, seq_devs, LANES), lambda s: (0, 0, 0)),
        out_shape=jax.ShapeDtypeStruct((team, seq_devs, LANES), F32),
        scratch_shapes=[pltpu.VMEM((seq_devs, slice_rows), F32)],
        compiler_params=params,
        name="part",
    )(lengths, posteriors)
    sums = lax.all_to_all(part, TEAM, split_axis=0, concat_axis=0, tiled=True)

    row_spec = pl.BlockSpec((1, rows), lambda s: (0, 0))
    send, tag = pl.pallas_call(
        functools.partial(bucket_kernel, rows, slots),
        grid=(seq_devs,),
        in_specs=[smem, row_spec, row_spec, x_spec],
        out_specs=[
            pl.BlockSpec((vocab_devs, CAP, chunk), lambda s: (s, 0, 0)),
            pl.BlockSpec((slots, LANES), lambda s: (0, 0)),
        ],
        out_shape=[
            jax.ShapeDtypeStruct((devs, CAP, chunk), BF16),
            jax.ShapeDtypeStruct((slots, LANES), F32),
        ],
        scratch_shapes=[pltpu.VMEM((slots, rows), BF16)],
        compiler_params=params,
        cost_estimate=pl.CostEstimate(
            flops=2 * slots * rows * states, bytes_accessed=8 * rows * states, transcendentals=0
        ),
        name="bucket",
    )(lengths, token_block.reshape(1, rows), token_offset.reshape(1, rows), posteriors)

    tail = slice_rows // LANES
    send = pl.pallas_call(
        functools.partial(carry_kernel, seq_devs, slots),
        grid=(1,),
        in_specs=[
            pl.BlockSpec((team, seq_devs, LANES), lambda i: (0, 0, 0)),
            pl.BlockSpec((slots, LANES), lambda i: (0, 0)),
            pl.BlockSpec(memory_space=pl.ANY),
        ],
        out_specs=pl.BlockSpec((devs, CAP, LANES), lambda i: (0, 0, tail)),
        out_shape=jax.ShapeDtypeStruct((devs, CAP, chunk), BF16),
        input_output_aliases={2: 0},
        compiler_params=params,
        name="carry",
    )(sums, tag, send)

    got = lax.all_to_all(send, SEQ + VOC, split_axis=0, concat_axis=0, tiled=True)

    cols = 2 * LANES
    dims = (seq_devs,) + tuple(lax.axis_size(a) for a in VOC)
    return pl.pallas_call(
        functools.partial(final_kernel, dims, ratio),
        grid=(slice_rows // cols,),
        in_specs=[
            pl.BlockSpec((tail, LANES), lambda p: (0, 0)),
            pl.BlockSpec((devs, CAP, cols), lambda p: (0, 0, p)),
            pl.BlockSpec((devs, CAP, LANES), lambda p: (0, 0, tail)),
        ],
        out_specs=pl.BlockSpec((cols, width), lambda p: (p, 0)),
        out_shape=jax.ShapeDtypeStruct((slice_rows, width), F32),
        scratch_shapes=[
            pltpu.VMEM((width, devs * CAP), BF16),
            pltpu.VMEM((tail, LANES), F32),
        ],
        compiler_params=params,
        name="final",
    )(smoothing.reshape(tail, LANES), got, got)


def solution(mesh):
    fine = Mesh(mesh.devices.reshape(4, 2, 8, 4, 2), SEQ + VOC)
    placed = (P(SEQ + VOC, None), P(SEQ + VOC, None), P(SEQ + VOC), P(), P(SEQ))
    return jax.shard_map(
        shards, mesh=fine, in_specs=placed, out_specs=P(SEQ, VOC), check_vma=False
    )
```

```python
import functools

import jax
import jax.numpy as jnp
from jax import lax
from jax.experimental import pallas as pl
from jax.experimental.pallas import tpu as pltpu
from jax.sharding import Mesh, PartitionSpec as P

VOCAB = 16384
SEQ = ("zlo", "core")
VOC = ("y", "x", "zhi")
TEAM = ("zlo", "core", "x")
LANES = 128
CAP = 2
HALF = 64
F32 = jnp.float32
BF16 = jnp.bfloat16
VMEM_LIMIT = 60 * 2**20


def live_rows(rows, lengths_ref):
    bound = lengths_ref[lax.axis_index(SEQ)] - lax.axis_index(VOC) * rows
    return lambda shape, dim: lax.broadcasted_iota(jnp.int32, shape, dim) < bound


def part_kernel(rows, seq_devs, slice_rows, lengths_ref, x_ref, o_ref, acc_ref):
    p = pl.program_id(0)
    each = x_ref.shape[1] // slice_rows
    shape = (seq_devs, rows)
    live = live_rows(rows, lengths_ref)(shape, 1)
    total = jnp.zeros((seq_devs, slice_rows), F32)
    for i in range(each):
        mine = lax.broadcasted_iota(jnp.int32, shape, 0) == p * each + i
        left = jnp.where(live & mine, 1.0, 0.0).astype(BF16)
        block = x_ref[:, i * slice_rows : (i + 1) * slice_rows]
        total = total + jnp.dot(left, block, preferred_element_type=F32)

    @pl.when(p == 0)
    def _():
        acc_ref[...] = total

    @pl.when(p > 0)
    def _():
        acc_ref[...] += total

    @pl.when(p == pl.num_programs(0) - 1)
    def _():
        for t in range(slice_rows // LANES):
            tile = acc_ref[:, t * LANES : (t + 1) * LANES]
            o_ref[2 * t] = tile
            o_ref[2 * t + 1] = pltpu.roll(tile, HALF, 1)


def bucket_kernel(rows, slots, lengths_ref, blk_ref, off_ref, x_ref, o_ref, tag_ref, pick_ref):
    n, each = o_ref.shape[:2]
    slice_rows = x_ref.shape[1] // each

    @pl.when(pl.program_id(0) == 0)
    def _():
        shape = (slots, rows)
        live = live_rows(rows, lengths_ref)(shape, 1)
        k = lax.broadcasted_iota(jnp.int32, shape, 0)
        hit = live & (blk_ref[...] == k // CAP)
        before = lax.broadcasted_iota(jnp.int32, (rows, rows), 0) < lax.broadcasted_iota(
            jnp.int32, (rows, rows), 1
        )
        rank = jnp.dot(
            jnp.where(hit, 1.0, 0.0).astype(BF16),
            jnp.where(before, 1.0, 0.0).astype(BF16),
            preferred_element_type=F32,
        )
        pick = hit & (rank == (k % CAP).astype(F32))
        pick_ref[...] = jnp.where(pick, 1.0, 0.0).astype(BF16)
        value = jnp.where(pick, (off_ref[...] + 1).astype(F32), 0.0)
        tag = jnp.sum(value, axis=1, keepdims=True) - 1.0
        lane = lax.broadcasted_iota(jnp.int32, (slots, LANES), 1)
        tag_ref[...] = jnp.where(lane == HALF, tag, 0.0)

    for i in range(each):
        block = x_ref[:, i * slice_rows : (i + 1) * slice_rows]
        y = jnp.dot(pick_ref[...], block, preferred_element_type=F32).astype(BF16)
        o_ref[:, i, :, :slice_rows] = y.reshape(n, CAP, slice_rows)


def carry_kernel(seq_devs, slots, sums_ref, tag_ref, send_ref, o_ref):
    del send_ref
    total = jnp.sum(sums_ref[...], axis=0)
    high = total.astype(BF16).astype(F32)
    low = total - high
    shape = (slots, LANES)
    odd = lax.broadcasted_iota(jnp.int32, shape, 0) % CAP == 1
    lane = lax.broadcasted_iota(jnp.int32, shape, 1)
    tag = tag_ref[...]
    n = slots // CAP
    for s in range(seq_devs):
        both = jnp.where(odd, low[s : s + 1], high[s : s + 1])
        carry = jnp.where(lane < HALF, both, tag).astype(BF16)
        o_ref[:, s] = carry.reshape(n, CAP, LANES)


def final_kernel(dims, ratio, smooth_ref, data_ref, carry_ref, o_ref, hot_ref, tot_ref):
    seq_devs, y_devs, x_devs, h_devs = dims
    p = pl.program_id(0)
    kk = seq_devs * y_devs * x_devs * h_devs * CAP
    width = o_ref.shape[1]
    cols = data_ref.shape[2]
    tiles = cols // LANES

    @pl.when(p == 0)
    def _():
        carry = carry_ref[...].reshape(kk, LANES)
        sel = lax.broadcasted_iota(jnp.int32, (16, LANES), 1) == HALF
        off = lax.dot_general(
            jnp.where(sel, 1.0, 0.0).astype(BF16),
            carry,
            (((1,), (1,)), ((), ())),
            preferred_element_type=F32,
        )[0:1]
        v = lax.broadcasted_iota(jnp.int32, (width, kk), 0).astype(F32)
        hot_ref[...] = jnp.where(off == v, 1.0, 0.0).astype(BF16)
        n = tot_ref.shape[0]
        k = lax.broadcasted_iota(jnp.int32, (n, kk), 1)
        member = (k // CAP) % seq_devs * x_devs + k // (CAP * seq_devs * h_devs) % x_devs
        t = lax.broadcasted_iota(jnp.int32, (n, kk), 0)
        even = jnp.where(member == 2 * t, 1.0, 0.0).astype(BF16)
        odd = jnp.where(member == 2 * t + 1, 1.0, 0.0).astype(BF16)
        even = jnp.dot(even, carry, preferred_element_type=F32)
        odd = jnp.dot(odd, carry, preferred_element_type=F32)
        lane = lax.broadcasted_iota(jnp.int32, (n, LANES), 1)
        tot_ref[...] = jnp.where(lane < HALF, even, pltpu.roll(odd, HALF, 1))

    counts = jnp.dot(hot_ref[...], data_ref[...].reshape(kk, cols), preferred_element_type=F32)
    for i in range(tiles):
        pseudo = smooth_ref[pl.ds(p * tiles + i, 1), :] * ratio
        scale = VOCAB / (tot_ref[pl.ds(p * tiles + i, 1), :] + VOCAB * pseudo)
        done = (counts[:, i * LANES : (i + 1) * LANES] + pseudo) * scale
        o_ref[i * LANES : (i + 1) * LANES, :] = done.T


def shards(posteriors, token_block, token_offset, lengths, smoothing):
    rows, states = posteriors.shape
    seq_devs = lax.axis_size(SEQ)
    vocab_devs = lax.axis_size(VOC)
    devs = seq_devs * vocab_devs
    team = lax.axis_size(TEAM)
    width = VOCAB // vocab_devs
    slice_rows = states // seq_devs
    slots = vocab_devs * CAP
    chunk = slice_rows + LANES
    ratio = rows * devs / VOCAB
    params = pltpu.CompilerParams(vmem_limit_bytes=VMEM_LIMIT)
    smem = pl.BlockSpec(memory_space=pltpu.SMEM)
    steps = 2
    each = seq_devs // steps
    x_spec = pl.BlockSpec((rows, slice_rows * each), lambda s: (0, s))

    part = pl.pallas_call(
        functools.partial(part_kernel, rows, seq_devs, slice_rows),
        grid=(steps,),
        in_specs=[smem, x_spec],
        out_specs=pl.BlockSpec((team, seq_devs, LANES), lambda s: (0, 0, 0)),
        out_shape=jax.ShapeDtypeStruct((team, seq_devs, LANES), F32),
        scratch_shapes=[pltpu.VMEM((seq_devs, slice_rows), F32)],
        compiler_params=params,
        name="part",
    )(lengths, posteriors)
    sums = lax.all_to_all(part, TEAM, split_axis=0, concat_axis=0, tiled=True)

    row_spec = pl.BlockSpec((1, rows), lambda s: (0, 0))
    send, tag = pl.pallas_call(
        functools.partial(bucket_kernel, rows, slots),
        grid=(steps,),
        in_specs=[smem, row_spec, row_spec, x_spec],
        out_specs=[
            pl.BlockSpec((vocab_devs, each, CAP, chunk), lambda s: (0, s, 0, 0)),
            pl.BlockSpec((slots, LANES), lambda s: (0, 0)),
        ],
        out_shape=[
            jax.ShapeDtypeStruct((vocab_devs, seq_devs, CAP, chunk), BF16),
            jax.ShapeDtypeStruct((slots, LANES), F32),
        ],
        scratch_shapes=[pltpu.VMEM((slots, rows), BF16)],
        compiler_params=params,
        cost_estimate=pl.CostEstimate(
            flops=2 * slots * rows * states, bytes_accessed=8 * rows * states, transcendentals=0
        ),
        name="bucket",
    )(lengths, token_block.reshape(1, rows), token_offset.reshape(1, rows), posteriors)

    tail = slice_rows // LANES
    send = pl.pallas_call(
        functools.partial(carry_kernel, seq_devs, slots),
        grid=(1,),
        in_specs=[
            pl.BlockSpec((team, seq_devs, LANES), lambda i: (0, 0, 0)),
            pl.BlockSpec((slots, LANES), lambda i: (0, 0)),
            pl.BlockSpec(memory_space=pl.ANY),
        ],
        out_specs=pl.BlockSpec((vocab_devs, seq_devs, CAP, LANES), lambda i: (0, 0, 0, tail)),
        out_shape=jax.ShapeDtypeStruct((vocab_devs, seq_devs, CAP, chunk), BF16),
        input_output_aliases={2: 0},
        compiler_params=params,
        name="carry",
    )(sums, tag, send)

    send = send.reshape(devs, CAP, chunk)
    got = lax.all_to_all(send, VOC + SEQ, split_axis=0, concat_axis=0, tiled=True)

    cols = slice_rows // 2
    dims = (seq_devs,) + tuple(lax.axis_size(a) for a in VOC)
    return pl.pallas_call(
        functools.partial(final_kernel, dims, ratio),
        grid=(slice_rows // cols,),
        in_specs=[
            pl.BlockSpec((tail, LANES), lambda p: (0, 0)),
            pl.BlockSpec((devs, CAP, cols), lambda p: (0, 0, p)),
            pl.BlockSpec((devs, CAP, LANES), lambda p: (0, 0, tail)),
        ],
        out_specs=pl.BlockSpec((cols, width), lambda p: (p, 0)),
        out_shape=jax.ShapeDtypeStruct((slice_rows, width), F32),
        scratch_shapes=[
            pltpu.VMEM((width, devs * CAP), BF16),
            pltpu.VMEM((tail, LANES), F32),
        ],
        compiler_params=params,
        name="final",
    )(smoothing.reshape(tail, LANES), got, got)


def solution(mesh):
    fine = Mesh(mesh.devices.reshape(4, 2, 8, 4, 2), SEQ + VOC)
    placed = (P(SEQ + VOC, None), P(SEQ + VOC, None), P(SEQ + VOC), P(), P(SEQ))
    return jax.shard_map(
        shards, mesh=fine, in_specs=placed, out_specs=P(SEQ, VOC), check_vma=False
    )
```

```python
import functools

import jax
import jax.numpy as jnp
from jax import lax
from jax.experimental import pallas as pl
from jax.experimental.pallas import tpu as pltpu
from jax.sharding import Mesh, PartitionSpec as P

VOCAB = 16384
SEQ = ("zlo", "core")
VOC = ("y", "x", "zhi")
TEAM = ("y", "x")
LANES = 128
SUB = 8
CAP = 2
HALF = 64
F32 = jnp.float32
BF16 = jnp.bfloat16
MIB = 2**20


def bucket_kernel(rows, slots, lengths_ref, blk_ref, off_ref, x_ref, o_ref, pick_ref, tag_ref):
    n, each = o_ref.shape[:2]
    slice_rows = x_ref.shape[1] // each
    bound = lengths_ref[lax.axis_index(SEQ)] - lax.axis_index(VOC) * rows

    @pl.when(pl.program_id(0) == 0)
    def _():
        shape = (slots, rows)
        live = lax.broadcasted_iota(jnp.int32, shape, 1) < bound
        k = lax.broadcasted_iota(jnp.int32, shape, 0)
        hit = live & (blk_ref[...] == k // CAP)
        before = lax.broadcasted_iota(jnp.int32, (rows, rows), 0) < lax.broadcasted_iota(
            jnp.int32, (rows, rows), 1
        )
        rank = jnp.dot(
            jnp.where(hit, 1.0, 0.0).astype(BF16),
            jnp.where(before, 1.0, 0.0).astype(BF16),
            preferred_element_type=F32,
        )
        pick = hit & (rank == (k % CAP).astype(F32))
        pick_ref[...] = jnp.where(pick, 1.0, 0.0).astype(BF16)
        value = jnp.where(pick, (off_ref[...] + 1).astype(F32), 0.0)
        tag = jnp.sum(value, axis=1, keepdims=True) - 1.0
        tag_ref[...] = jnp.broadcast_to(tag, (slots, LANES))

    live = lax.broadcasted_iota(jnp.int32, (SUB, rows), 1) < bound
    left = jnp.where(live, 1.0, 0.0).astype(BF16)
    row = lax.broadcasted_iota(jnp.int32, (SUB, LANES), 0)
    lane = lax.broadcasted_iota(jnp.int32, (SUB, LANES), 1)
    for i in range(each):
        block = x_ref[:, i * slice_rows : (i + 1) * slice_rows]
        y = jnp.dot(pick_ref[...], block, preferred_element_type=F32).astype(BF16)
        o_ref[:, i, :, :slice_rows] = y.reshape(n, CAP, slice_rows)
        part = jnp.dot(left, block, preferred_element_type=F32)
        tiles = []
        for t in range(slots // SUB):
            mine = part[:, t * LANES : (t + 1) * LANES]
            mine = jnp.where(row < SUB // 2, mine, pltpu.roll(mine, HALF, 1))
            high = mine.astype(BF16).astype(F32)
            both = jnp.where(row % CAP == 0, high, mine - high)
            tag = tag_ref[t * SUB : (t + 1) * SUB, :]
            tiles.append(jnp.where(lane < HALF, both, tag))
        carry = jnp.concatenate(tiles, axis=0).astype(BF16)
        o_ref[:, i, :, slice_rows:] = carry.reshape(n, CAP, LANES)


def total_kernel(carry_ref, o_ref):
    carry = carry_ref[...].reshape(-1, LANES)
    ones = jnp.ones((SUB, carry.shape[0]), BF16)
    total = jnp.dot(ones, carry, preferred_element_type=F32)
    for m in range(o_ref.shape[0]):
        o_ref[m] = total


def count_kernel(data_ref, carry_ref, o_ref, hot_ref):
    kk = hot_ref.shape[1]
    width = hot_ref.shape[0]

    @pl.when(pl.program_id(0) == 0)
    def _():
        sel = lax.broadcasted_iota(jnp.int32, (16, LANES), 1) == HALF
        off = lax.dot_general(
            jnp.where(sel, 1.0, 0.0).astype(BF16),
            carry_ref[...].reshape(kk, LANES),
            (((1,), (1,)), ((), ())),
            preferred_element_type=F32,
        )[0:1]
        v = lax.broadcasted_iota(jnp.int32, (width, kk), 0).astype(F32)
        hot_ref[...] = jnp.where(off == v, 1.0, 0.0).astype(BF16)

    data = data_ref[...].reshape(kk, data_ref.shape[2])
    o_ref[...] = jnp.dot(hot_ref[...], data, preferred_element_type=F32)


def scale_kernel(ratio, smooth_ref, totals_ref, counts_ref, o_ref):
    tiles = counts_ref.shape[1] // LANES
    first = pl.program_id(0) * tiles
    lane = lax.broadcasted_iota(jnp.int32, (1, LANES), 1)
    for i in range(tiles):
        t = first + i
        even = totals_ref[2 * t, 0:1, :]
        odd = totals_ref[2 * t + 1, 0:1, :]
        total = jnp.where(lane < HALF, even, pltpu.roll(odd, HALF, 1))
        pseudo = smooth_ref[pl.ds(t, 1), :] * ratio
        scale = VOCAB / (total + VOCAB * pseudo)
        done = (counts_ref[:, i * LANES : (i + 1) * LANES] + pseudo) * scale
        o_ref[i * LANES : (i + 1) * LANES, :] = done.T


def shards(posteriors, token_block, token_offset, lengths, smoothing):
    rows, states = posteriors.shape
    seq_devs = lax.axis_size(SEQ)
    vocab_devs = lax.axis_size(VOC)
    devs = seq_devs * vocab_devs
    team = lax.axis_size(TEAM)
    width = VOCAB // vocab_devs
    slice_rows = states // seq_devs
    slots = vocab_devs * CAP
    chunk = slice_rows + LANES
    ratio = rows * devs / VOCAB
    steps = 2
    each = seq_devs // steps
    tail = slice_rows // LANES
    params = pltpu.CompilerParams(vmem_limit_bytes=60 * MIB)

    row_spec = pl.BlockSpec((1, rows), lambda s: (0, 0))
    send = pl.pallas_call(
        functools.partial(bucket_kernel, rows, slots),
        grid=(steps,),
        in_specs=[
            pl.BlockSpec(memory_space=pltpu.SMEM),
            row_spec,
            row_spec,
            pl.BlockSpec((rows, slice_rows * each), lambda s: (0, s)),
        ],
        out_specs=pl.BlockSpec((vocab_devs, each, CAP, chunk), lambda s: (0, s, 0, 0)),
        out_shape=jax.ShapeDtypeStruct((vocab_devs, seq_devs, CAP, chunk), BF16),
        scratch_shapes=[pltpu.VMEM((slots, rows), BF16), pltpu.VMEM((slots, LANES), F32)],
        compiler_params=pltpu.CompilerParams(vmem_limit_bytes=46 * MIB),
        name="bucket",
    )(lengths, token_block.reshape(1, rows), token_offset.reshape(1, rows), posteriors)

    send = send.reshape(devs, CAP, chunk)
    got = lax.all_to_all(send, VOC + SEQ, split_axis=0, concat_axis=0, tiled=True)

    carry_spec = pl.BlockSpec((devs, CAP, LANES), lambda p: (0, 0, tail))
    mine = pl.pallas_call(
        total_kernel,
        grid=(1,),
        in_specs=[carry_spec],
        out_specs=pl.BlockSpec((team, SUB, LANES), lambda i: (0, 0, 0)),
        out_shape=jax.ShapeDtypeStruct((team, SUB, LANES), F32),
        compiler_params=params,
        name="total",
    )(got)
    totals = lax.all_to_all(mine, TEAM, split_axis=0, concat_axis=0, tiled=True)

    cols = slice_rows // 2
    counts = pl.pallas_call(
        count_kernel,
        grid=(slice_rows // cols,),
        in_specs=[pl.BlockSpec((devs, CAP, cols), lambda p: (0, 0, p)), carry_spec],
        out_specs=pl.BlockSpec((width, cols), lambda p: (0, p)),
        out_shape=jax.ShapeDtypeStruct((width, slice_rows), F32),
        scratch_shapes=[pltpu.VMEM((width, devs * CAP), BF16)],
        compiler_params=params,
        cost_estimate=pl.CostEstimate(
            flops=2 * devs * CAP * width * slice_rows,
            bytes_accessed=2 * devs * CAP * chunk + 4 * width * slice_rows,
            transcendentals=0,
        ),
        name="count",
    )(got, got)

    return pl.pallas_call(
        functools.partial(scale_kernel, ratio),
        grid=(slice_rows // cols,),
        in_specs=[
            pl.BlockSpec((tail, LANES), lambda p: (0, 0)),
            pl.BlockSpec((team, SUB, LANES), lambda p: (0, 0, 0)),
            pl.BlockSpec((width, cols), lambda p: (0, p)),
        ],
        out_specs=pl.BlockSpec((cols, width), lambda p: (p, 0)),
        out_shape=jax.ShapeDtypeStruct((slice_rows, width), F32),
        compiler_params=params,
        name="scale",
    )(smoothing.reshape(tail, LANES), totals, counts)


def solution(mesh):
    fine = Mesh(mesh.devices.reshape(4, 2, 8, 4, 2), SEQ + VOC)
    placed = (P(SEQ + VOC, None), P(SEQ + VOC, None), P(SEQ + VOC), P(), P(SEQ))
    return jax.shard_map(
        shards, mesh=fine, in_specs=placed, out_specs=P(SEQ, VOC), check_vma=False
    )
```

```python
import functools

import jax
import jax.numpy as jnp
from jax import lax
from jax.experimental import pallas as pl
from jax.experimental.pallas import tpu as pltpu
from jax.sharding import Mesh, PartitionSpec as P

VOCAB = 16384
SEQ = ("zlo", "core")
VOC = ("y", "x", "zhi")
TEAM = ("zlo", "core", "x")
LANES = 128
CAP = 2
HALF = 64
F32 = jnp.float32
BF16 = jnp.bfloat16
VMEM_LIMIT = 60 * 2**20


def live_rows(rows, lengths_ref):
    bound = lengths_ref[lax.axis_index(SEQ)] - lax.axis_index(VOC) * rows
    return lambda shape, dim: lax.broadcasted_iota(jnp.int32, shape, dim) < bound


def part_kernel(rows, seq_devs, slice_rows, lengths_ref, x_ref, o_ref, acc_ref):
    p = pl.program_id(0)
    each = x_ref.shape[1] // slice_rows
    shape = (seq_devs, rows)
    live = live_rows(rows, lengths_ref)(shape, 1)
    total = jnp.zeros((seq_devs, slice_rows), F32)
    for i in range(each):
        mine = lax.broadcasted_iota(jnp.int32, shape, 0) == p * each + i
        left = jnp.where(live & mine, 1.0, 0.0).astype(BF16)
        block = x_ref[:, i * slice_rows : (i + 1) * slice_rows]
        total = total + jnp.dot(left, block, preferred_element_type=F32)

    @pl.when(p == 0)
    def _():
        acc_ref[...] = total

    @pl.when(p > 0)
    def _():
        acc_ref[...] += total

    @pl.when(p == pl.num_programs(0) - 1)
    def _():
        for t in range(slice_rows // LANES):
            tile = acc_ref[:, t * LANES : (t + 1) * LANES]
            o_ref[2 * t] = tile
            o_ref[2 * t + 1] = pltpu.roll(tile, HALF, 1)


def bucket_kernel(rows, slots, lengths_ref, blk_ref, off_ref, x_ref, o_ref, tag_ref, pick_ref):
    n, each = o_ref.shape[:2]
    slice_rows = x_ref.shape[1] // each

    @pl.when(pl.program_id(0) == 0)
    def _():
        shape = (slots, rows)
        live = live_rows(rows, lengths_ref)(shape, 1)
        k = lax.broadcasted_iota(jnp.int32, shape, 0)
        hit = live & (blk_ref[...] == k // CAP)
        before = lax.broadcasted_iota(jnp.int32, (rows, rows), 0) < lax.broadcasted_iota(
            jnp.int32, (rows, rows), 1
        )
        rank = jnp.dot(
            jnp.where(hit, 1.0, 0.0).astype(BF16),
            jnp.where(before, 1.0, 0.0).astype(BF16),
            preferred_element_type=F32,
        )
        pick = hit & (rank == (k % CAP).astype(F32))
        pick_ref[...] = jnp.where(pick, 1.0, 0.0).astype(BF16)
        value = jnp.where(pick, (off_ref[...] + 1).astype(F32), 0.0)
        tag = jnp.sum(value, axis=1, keepdims=True) - 1.0
        lane = lax.broadcasted_iota(jnp.int32, (slots, LANES), 1)
        tag_ref[...] = jnp.where(lane == HALF, tag, 0.0)

    for i in range(each):
        block = x_ref[:, i * slice_rows : (i + 1) * slice_rows]
        y = jnp.dot(pick_ref[...], block, preferred_element_type=F32).astype(BF16)
        o_ref[:, i, :, :slice_rows] = y.reshape(n, CAP, slice_rows)


def carry_kernel(seq_devs, slots, sums_ref, tag_ref, send_ref, o_ref):
    del send_ref
    total = jnp.sum(sums_ref[...], axis=0)
    high = total.astype(BF16).astype(F32)
    low = total - high
    shape = (slots, LANES)
    odd = lax.broadcasted_iota(jnp.int32, shape, 0) % CAP == 1
    lane = lax.broadcasted_iota(jnp.int32, shape, 1)
    tag = tag_ref[...]
    n = slots // CAP
    for s in range(seq_devs):
        both = jnp.where(odd, low[s : s + 1], high[s : s + 1])
        carry = jnp.where(lane < HALF, both, tag).astype(BF16)
        o_ref[:, s] = carry.reshape(n, CAP, LANES)


def final_kernel(dims, ratio, smooth_ref, got_ref, o_ref, hot_ref, tot_ref):
    seq_devs, y_devs, x_devs, h_devs = dims
    p = pl.program_id(0)
    kk = seq_devs * y_devs * x_devs * h_devs * CAP
    cols, width = o_ref.shape
    tiles = cols // LANES
    slice_rows = got_ref.shape[2] - LANES

    @pl.when(p == 0)
    def _():
        carry = got_ref[:, :, slice_rows:].reshape(kk, LANES)
        sel = lax.broadcasted_iota(jnp.int32, (16, LANES), 1) == HALF
        off = lax.dot_general(
            jnp.where(sel, 1.0, 0.0).astype(BF16),
            carry,
            (((1,), (1,)), ((), ())),
            preferred_element_type=F32,
        )[0:1]
        v = lax.broadcasted_iota(jnp.int32, (width, kk), 0).astype(F32)
        hot_ref[...] = jnp.where(off == v, 1.0, 0.0).astype(BF16)
        n = tot_ref.shape[0]
        k = lax.broadcasted_iota(jnp.int32, (n, kk), 1)
        member = (k // CAP) % seq_devs * x_devs + k // (CAP * seq_devs * h_devs) % x_devs
        t = lax.broadcasted_iota(jnp.int32, (n, kk), 0)
        even = jnp.where(member == 2 * t, 1.0, 0.0).astype(BF16)
        odd = jnp.where(member == 2 * t + 1, 1.0, 0.0).astype(BF16)
        even = jnp.dot(even, carry, preferred_element_type=F32)
        odd = jnp.dot(odd, carry, preferred_element_type=F32)
        lane = lax.broadcasted_iota(jnp.int32, (n, LANES), 1)
        tot_ref[...] = jnp.where(lane < HALF, even, pltpu.roll(odd, HALF, 1))

    data = got_ref[:, :, pl.ds(pl.multiple_of(p * cols, LANES), cols)].reshape(kk, cols)
    counts = jnp.dot(hot_ref[...], data, preferred_element_type=F32)
    for i in range(tiles):
        pseudo = smooth_ref[pl.ds(p * tiles + i, 1), :] * ratio
        scale = VOCAB / (tot_ref[pl.ds(p * tiles + i, 1), :] + VOCAB * pseudo)
        done = (counts[:, i * LANES : (i + 1) * LANES] + pseudo) * scale
        o_ref[i * LANES : (i + 1) * LANES, :] = done.T


def shards(posteriors, token_block, token_offset, lengths, smoothing):
    rows, states = posteriors.shape
    seq_devs = lax.axis_size(SEQ)
    vocab_devs = lax.axis_size(VOC)
    devs = seq_devs * vocab_devs
    team = lax.axis_size(TEAM)
    width = VOCAB // vocab_devs
    slice_rows = states // seq_devs
    slots = vocab_devs * CAP
    chunk = slice_rows + LANES
    ratio = rows * devs / VOCAB
    params = pltpu.CompilerParams(vmem_limit_bytes=VMEM_LIMIT)
    smem = pl.BlockSpec(memory_space=pltpu.SMEM)
    steps = 2
    each = seq_devs // steps
    x_spec = pl.BlockSpec((rows, slice_rows * each), lambda s: (0, s))

    part = pl.pallas_call(
        functools.partial(part_kernel, rows, seq_devs, slice_rows),
        grid=(steps,),
        in_specs=[smem, x_spec],
        out_specs=pl.BlockSpec((team, seq_devs, LANES), lambda s: (0, 0, 0)),
        out_shape=jax.ShapeDtypeStruct((team, seq_devs, LANES), F32),
        scratch_shapes=[pltpu.VMEM((seq_devs, slice_rows), F32)],
        compiler_params=params,
        name="part",
    )(lengths, posteriors)
    sums = lax.all_to_all(part, TEAM, split_axis=0, concat_axis=0, tiled=True)

    row_spec = pl.BlockSpec((1, rows), lambda s: (0, 0))
    send, tag = pl.pallas_call(
        functools.partial(bucket_kernel, rows, slots),
        grid=(steps,),
        in_specs=[smem, row_spec, row_spec, x_spec],
        out_specs=[
            pl.BlockSpec((vocab_devs, each, CAP, chunk), lambda s: (0, s, 0, 0)),
            pl.BlockSpec((slots, LANES), lambda s: (0, 0)),
        ],
        out_shape=[
            jax.ShapeDtypeStruct((vocab_devs, seq_devs, CAP, chunk), BF16),
            jax.ShapeDtypeStruct((slots, LANES), F32),
        ],
        scratch_shapes=[pltpu.VMEM((slots, rows), BF16)],
        compiler_params=params,
        cost_estimate=pl.CostEstimate(
            flops=2 * slots * rows * states, bytes_accessed=8 * rows * states, transcendentals=0
        ),
        name="bucket",
    )(lengths, token_block.reshape(1, rows), token_offset.reshape(1, rows), posteriors)

    tail = slice_rows // LANES
    send = pl.pallas_call(
        functools.partial(carry_kernel, seq_devs, slots),
        grid=(1,),
        in_specs=[
            pl.BlockSpec((team, seq_devs, LANES), lambda i: (0, 0, 0)),
            pl.BlockSpec((slots, LANES), lambda i: (0, 0)),
            pl.BlockSpec(memory_space=pl.ANY),
        ],
        out_specs=pl.BlockSpec((vocab_devs, seq_devs, CAP, LANES), lambda i: (0, 0, 0, tail)),
        out_shape=jax.ShapeDtypeStruct((vocab_devs, seq_devs, CAP, chunk), BF16),
        input_output_aliases={2: 0},
        compiler_params=pltpu.CompilerParams(vmem_limit_bytes=60 * 2**20),
        name="carry",
    )(sums, tag, send)

    send = send.reshape(devs, CAP, chunk)
    got = lax.all_to_all(send, VOC + SEQ, split_axis=0, concat_axis=0, tiled=True)

    cols = slice_rows // 2
    dims = (seq_devs,) + tuple(lax.axis_size(a) for a in VOC)
    return pl.pallas_call(
        functools.partial(final_kernel, dims, ratio),
        grid=(slice_rows // cols,),
        in_specs=[
            pl.BlockSpec((tail, LANES), lambda p: (0, 0)),
            pl.BlockSpec(memory_space=pltpu.VMEM),
        ],
        out_specs=pl.BlockSpec((cols, width), lambda p: (p, 0)),
        out_shape=jax.ShapeDtypeStruct((slice_rows, width), F32),
        scratch_shapes=[
            pltpu.VMEM((width, devs * CAP), BF16),
            pltpu.VMEM((tail, LANES), F32),
        ],
        compiler_params=pltpu.CompilerParams(vmem_limit_bytes=32 * 2**20),
        name="final",
    )(smoothing.reshape(tail, LANES), got)


def solution(mesh):
    fine = Mesh(mesh.devices.reshape(4, 2, 8, 4, 2), SEQ + VOC)
    placed = (P(SEQ + VOC, None), P(SEQ + VOC, None), P(SEQ + VOC), P(), P(SEQ))
    return jax.shard_map(
        shards, mesh=fine, in_specs=placed, out_specs=P(SEQ, VOC), check_vma=False
    )
```

```python
import functools

import jax
import jax.numpy as jnp
from jax import lax
from jax.experimental import pallas as pl
from jax.experimental.pallas import tpu as pltpu
from jax.sharding import Mesh, PartitionSpec as P

VOCAB = 16384
SEQ = ("z1", "z0", "core")
VOC = ("yh", "yl", "x", "zhi")
TEAM = ("z0", "core", "yl", "x")
LANES = 128
CAP = 2
HALF = 64
F32 = jnp.float32
BF16 = jnp.bfloat16
VMEM_LIMIT = 60 * 2**20


def live_rows(rows, lengths_ref):
    bound = lengths_ref[lax.axis_index(SEQ)] - lax.axis_index(VOC) * rows
    return lambda shape, dim: lax.broadcasted_iota(jnp.int32, shape, dim) < bound


def part_kernel(rows, seq_devs, slice_rows, lengths_ref, x_ref, o_ref, acc_ref):
    p = pl.program_id(0)
    each = x_ref.shape[1] // slice_rows
    shape = (seq_devs, rows)
    live = live_rows(rows, lengths_ref)(shape, 1)
    total = jnp.zeros((seq_devs, slice_rows), F32)
    for i in range(each):
        mine = lax.broadcasted_iota(jnp.int32, shape, 0) == p * each + i
        left = jnp.where(live & mine, 1.0, 0.0).astype(BF16)
        block = x_ref[:, i * slice_rows : (i + 1) * slice_rows]
        total = total + jnp.dot(left, block, preferred_element_type=F32)

    @pl.when(p == 0)
    def _():
        acc_ref[...] = total

    @pl.when(p > 0)
    def _():
        acc_ref[...] += total

    @pl.when(p == pl.num_programs(0) - 1)
    def _():
        n = seq_devs // 2
        lane = lax.broadcasted_iota(jnp.int32, (n, LANES), 1)
        for t in range(slice_rows // LANES):
            tile = acc_ref[:, t * LANES : (t + 1) * LANES]
            turned = pltpu.roll(tile, HALF, 1)
            o_ref[2 * t] = jnp.where(lane < HALF, tile[:n], turned[n:])
            o_ref[2 * t + 1] = jnp.where(lane < HALF, turned[:n], tile[n:])


def bucket_kernel(rows, slots, lengths_ref, blk_ref, off_ref, x_ref, o_ref, tag_ref, pick_ref):
    n, each = o_ref.shape[:2]
    slice_rows = x_ref.shape[1] // each

    @pl.when(pl.program_id(0) == 0)
    def _():
        shape = (slots, rows)
        live = live_rows(rows, lengths_ref)(shape, 1)
        k = lax.broadcasted_iota(jnp.int32, shape, 0)
        hit = live & (blk_ref[...] == k // CAP)
        before = lax.broadcasted_iota(jnp.int32, (rows, rows), 0) < lax.broadcasted_iota(
            jnp.int32, (rows, rows), 1
        )
        rank = jnp.dot(
            jnp.where(hit, 1.0, 0.0).astype(BF16),
            jnp.where(before, 1.0, 0.0).astype(BF16),
            preferred_element_type=F32,
        )
        pick = hit & (rank == (k % CAP).astype(F32))
        pick_ref[...] = jnp.where(pick, 1.0, 0.0).astype(BF16)
        value = jnp.where(pick, (off_ref[...] + 1).astype(F32), 0.0)
        tag = jnp.sum(value, axis=1, keepdims=True) - 1.0
        lane = lax.broadcasted_iota(jnp.int32, (slots, LANES), 1)
        tag_ref[...] = jnp.where(lane == HALF, tag, 0.0)

    for i in range(each):
        block = x_ref[:, i * slice_rows : (i + 1) * slice_rows]
        y = jnp.dot(pick_ref[...], block, preferred_element_type=F32).astype(BF16)
        o_ref[:, i, :, :slice_rows] = y.reshape(n, CAP, slice_rows)


def carry_kernel(seq_devs, slots, sums_ref, tag_ref, send_ref, o_ref):
    del send_ref
    total = jnp.sum(sums_ref[...], axis=0)
    total = jnp.concatenate([total, pltpu.roll(total, HALF, 1)], axis=0)
    high = total.astype(BF16).astype(F32)
    low = total - high
    shape = (slots, LANES)
    odd = lax.broadcasted_iota(jnp.int32, shape, 0) % CAP == 1
    lane = lax.broadcasted_iota(jnp.int32, shape, 1)
    tag = tag_ref[...]
    n = slots // CAP
    for s in range(seq_devs):
        both = jnp.where(odd, low[s : s + 1], high[s : s + 1])
        carry = jnp.where(lane < HALF, both, tag).astype(BF16)
        o_ref[:, s] = carry.reshape(n, CAP, LANES)


def final_kernel(seq_devs, team_axes, ratio, smooth_ref, got_ref, o_ref, hot_ref, tot_ref):
    team_seq, team_voc, h_devs = team_axes
    p = pl.program_id(0)
    kk = got_ref.shape[0] * CAP
    cols, width = o_ref.shape
    tiles = cols // LANES
    slice_rows = got_ref.shape[2] - LANES

    @pl.when(p == 0)
    def _():
        carry = got_ref[:, :, slice_rows:].reshape(kk, LANES)
        sel = lax.broadcasted_iota(jnp.int32, (16, LANES), 1) == HALF
        off = lax.dot_general(
            jnp.where(sel, 1.0, 0.0).astype(BF16),
            carry,
            (((1,), (1,)), ((), ())),
            preferred_element_type=F32,
        )[0:1]
        v = lax.broadcasted_iota(jnp.int32, (width, kk), 0).astype(F32)
        hot_ref[...] = jnp.where(off == v, 1.0, 0.0).astype(BF16)
        n = tot_ref.shape[0]
        k = lax.broadcasted_iota(jnp.int32, (n, kk), 1)
        member = k // CAP % team_seq * team_voc + k // (CAP * seq_devs * h_devs) % team_voc
        t = lax.broadcasted_iota(jnp.int32, (n, kk), 0)
        even = jnp.where(member == 2 * t, 1.0, 0.0).astype(BF16)
        odd = jnp.where(member == 2 * t + 1, 1.0, 0.0).astype(BF16)
        even = jnp.dot(even, carry, preferred_element_type=F32)
        odd = jnp.dot(odd, carry, preferred_element_type=F32)
        lane = lax.broadcasted_iota(jnp.int32, (n, LANES), 1)
        tot_ref[...] = jnp.where(lane < HALF, even, pltpu.roll(odd, HALF, 1))

    data = got_ref[:, :, pl.ds(pl.multiple_of(p * cols, LANES), cols)].reshape(kk, cols)
    counts = jnp.dot(hot_ref[...], data, preferred_element_type=F32)
    for i in range(tiles):
        pseudo = smooth_ref[pl.ds(p * tiles + i, 1), :] * ratio
        scale = VOCAB / (tot_ref[pl.ds(p * tiles + i, 1), :] + VOCAB * pseudo)
        done = (counts[:, i * LANES : (i + 1) * LANES] + pseudo) * scale
        o_ref[i * LANES : (i + 1) * LANES, :] = done.T


def shards(posteriors, token_block, token_offset, lengths, smoothing):
    rows, states = posteriors.shape
    seq_devs = lax.axis_size(SEQ)
    vocab_devs = lax.axis_size(VOC)
    devs = seq_devs * vocab_devs
    team = lax.axis_size(TEAM)
    width = VOCAB // vocab_devs
    slice_rows = states // seq_devs
    slots = vocab_devs * CAP
    chunk = slice_rows + LANES
    ratio = rows * devs / VOCAB
    params = pltpu.CompilerParams(vmem_limit_bytes=VMEM_LIMIT)
    smem = pl.BlockSpec(memory_space=pltpu.SMEM)
    steps = 2
    each = seq_devs // steps
    x_spec = pl.BlockSpec((rows, slice_rows * each), lambda s: (0, s))

    part = pl.pallas_call(
        functools.partial(part_kernel, rows, seq_devs, slice_rows),
        grid=(steps,),
        in_specs=[smem, x_spec],
        out_specs=pl.BlockSpec((team, seq_devs // 2, LANES), lambda s: (0, 0, 0)),
        out_shape=jax.ShapeDtypeStruct((team, seq_devs // 2, LANES), F32),
        scratch_shapes=[pltpu.VMEM((seq_devs, slice_rows), F32)],
        compiler_params=params,
        name="part",
    )(lengths, posteriors)
    sums = lax.all_to_all(part, TEAM, split_axis=0, concat_axis=0, tiled=True)

    row_spec = pl.BlockSpec((1, rows), lambda s: (0, 0))
    send, tag = pl.pallas_call(
        functools.partial(bucket_kernel, rows, slots),
        grid=(steps,),
        in_specs=[smem, row_spec, row_spec, x_spec],
        out_specs=[
            pl.BlockSpec((vocab_devs, each, CAP, chunk), lambda s: (0, s, 0, 0)),
            pl.BlockSpec((slots, LANES), lambda s: (0, 0)),
        ],
        out_shape=[
            jax.ShapeDtypeStruct((vocab_devs, seq_devs, CAP, chunk), BF16),
            jax.ShapeDtypeStruct((slots, LANES), F32),
        ],
        scratch_shapes=[pltpu.VMEM((slots, rows), BF16)],
        compiler_params=params,
        cost_estimate=pl.CostEstimate(
            flops=2 * slots * rows * states, bytes_accessed=8 * rows * states, transcendentals=0
        ),
        name="bucket",
    )(lengths, token_block.reshape(1, rows), token_offset.reshape(1, rows), posteriors)

    tail = slice_rows // LANES
    send = pl.pallas_call(
        functools.partial(carry_kernel, seq_devs, slots),
        grid=(1,),
        in_specs=[
            pl.BlockSpec((team, seq_devs // 2, LANES), lambda i: (0, 0, 0)),
            pl.BlockSpec((slots, LANES), lambda i: (0, 0)),
            pl.BlockSpec(memory_space=pl.ANY),
        ],
        out_specs=pl.BlockSpec((vocab_devs, seq_devs, CAP, LANES), lambda i: (0, 0, 0, tail)),
        out_shape=jax.ShapeDtypeStruct((vocab_devs, seq_devs, CAP, chunk), BF16),
        input_output_aliases={2: 0},
        compiler_params=pltpu.CompilerParams(vmem_limit_bytes=60 * 2**20),
        name="carry",
    )(sums, tag, send)

    send = send.reshape(devs, CAP, chunk)
    got = lax.all_to_all(send, VOC + SEQ, split_axis=0, concat_axis=0, tiled=True)

    cols = slice_rows // 2
    team_axes = (lax.axis_size(TEAM[:2]), lax.axis_size(TEAM[2:]), lax.axis_size(VOC[-1]))
    return pl.pallas_call(
        functools.partial(final_kernel, seq_devs, team_axes, ratio),
        grid=(slice_rows // cols,),
        in_specs=[
            pl.BlockSpec((tail, LANES), lambda p: (0, 0)),
            pl.BlockSpec(memory_space=pltpu.VMEM),
        ],
        out_specs=pl.BlockSpec((cols, width), lambda p: (p, 0)),
        out_shape=jax.ShapeDtypeStruct((slice_rows, width), F32),
        scratch_shapes=[
            pltpu.VMEM((width, devs * CAP), BF16),
            pltpu.VMEM((tail, LANES), F32),
        ],
        compiler_params=pltpu.CompilerParams(vmem_limit_bytes=32 * 2**20),
        name="final",
    )(smoothing.reshape(tail, LANES), got)


def solution(mesh):
    fine = Mesh(mesh.devices.reshape(2, 2, 2, 4, 2, 4, 2), SEQ + VOC)
    placed = (P(SEQ + VOC, None), P(SEQ + VOC, None), P(SEQ + VOC), P(), P(SEQ))
    return jax.shard_map(
        shards, mesh=fine, in_specs=placed, out_specs=P(SEQ, VOC), check_vma=False
    )
```

```python
import functools

import jax
import jax.numpy as jnp
from jax import lax
from jax.experimental import pallas as pl
from jax.experimental.pallas import tpu as pltpu
from jax.sharding import Mesh, PartitionSpec as P

VOCAB = 16384
SEQ = ("z1", "z0", "core")
VOC = ("yh", "yl", "x", "zhi")
TEAM = ("z0", "core", "yl", "x")
LANES = 128
CAP = 2
HALF = 64
F32 = jnp.float32
BF16 = jnp.bfloat16
VMEM_LIMIT = 60 * 2**20


def live_rows(rows, lengths_ref):
    bound = lengths_ref[lax.axis_index(SEQ)] - lax.axis_index(VOC) * rows
    return lambda shape, dim: lax.broadcasted_iota(jnp.int32, shape, dim) < bound


def part_kernel(rows, seq_devs, slice_rows, lengths_ref, x_ref, o_ref, acc_ref):
    p = pl.program_id(0)
    each = x_ref.shape[1] // slice_rows
    shape = (seq_devs, rows)
    live = live_rows(rows, lengths_ref)(shape, 1)
    total = jnp.zeros((seq_devs, slice_rows), F32)
    for i in range(each):
        mine = lax.broadcasted_iota(jnp.int32, shape, 0) == p * each + i
        left = jnp.where(live & mine, 1.0, 0.0).astype(BF16)
        block = x_ref[:, i * slice_rows : (i + 1) * slice_rows]
        total = total + jnp.dot(left, block, preferred_element_type=F32)

    @pl.when(p == 0)
    def _():
        acc_ref[...] = total

    @pl.when(p > 0)
    def _():
        acc_ref[...] += total

    @pl.when(p == pl.num_programs(0) - 1)
    def _():
        n = seq_devs // 2
        lane = lax.broadcasted_iota(jnp.int32, (n, LANES), 1)
        for t in range(slice_rows // LANES):
            tile = acc_ref[:, t * LANES : (t + 1) * LANES]
            turned = pltpu.roll(tile, HALF, 1)
            o_ref[2 * t] = jnp.where(lane < HALF, tile[:n], turned[n:])
            o_ref[2 * t + 1] = jnp.where(lane < HALF, turned[:n], tile[n:])


def bucket_kernel(rows, slots, lengths_ref, blk_ref, off_ref, x_ref, o_ref, pick_ref):
    n, each = o_ref.shape[:2]
    slice_rows = x_ref.shape[1] // each

    @pl.when(pl.program_id(0) == 0)
    def _():
        shape = (slots, rows)
        live = live_rows(rows, lengths_ref)(shape, 1)
        k = lax.broadcasted_iota(jnp.int32, shape, 0)
        hit = live & (blk_ref[...] == k // CAP)
        before = lax.broadcasted_iota(jnp.int32, (rows, rows), 0) < lax.broadcasted_iota(
            jnp.int32, (rows, rows), 1
        )
        rank = jnp.dot(
            jnp.where(hit, 1.0, 0.0).astype(BF16),
            jnp.where(before, 1.0, 0.0).astype(BF16),
            preferred_element_type=F32,
        )
        pick = hit & (rank == (k % CAP).astype(F32))
        pick_ref[...] = jnp.where(pick, 1.0, 0.0).astype(BF16)
        value = jnp.where(pick, (off_ref[...] + 1).astype(F32), 0.0)
        tag = jnp.sum(value, axis=1, keepdims=True) - 1.0
        lane = lax.broadcasted_iota(jnp.int32, (slots, LANES), 1)
        tag = jnp.where(lane == HALF, tag, 0.0).astype(BF16)
        o_ref[:, 0, :, slice_rows:] = tag.reshape(n, CAP, LANES)

    for i in range(each):
        block = x_ref[:, i * slice_rows : (i + 1) * slice_rows]
        y = jnp.dot(pick_ref[...], block, preferred_element_type=F32).astype(BF16)
        o_ref[:, i, :, :slice_rows] = y.reshape(n, CAP, slice_rows)


def carry_kernel(seq_devs, slots, sums_ref, tag_ref, o_ref):
    total = jnp.sum(sums_ref[...], axis=0)
    total = jnp.concatenate([total, pltpu.roll(total, HALF, 1)], axis=0)
    high = total.astype(BF16).astype(F32)
    low = total - high
    shape = (slots, LANES)
    odd = lax.broadcasted_iota(jnp.int32, shape, 0) % CAP == 1
    lane = lax.broadcasted_iota(jnp.int32, shape, 1)
    tag = tag_ref[...].reshape(slots, LANES).astype(F32)
    n = slots // CAP
    for s in range(seq_devs):
        both = jnp.where(odd, low[s : s + 1], high[s : s + 1])
        carry = jnp.where(lane < HALF, both, tag).astype(BF16)
        o_ref[:, s] = carry.reshape(n, CAP, LANES)


def final_kernel(seq_devs, team_axes, ratio, smooth_ref, got_ref, o_ref, hot_ref, tot_ref):
    team_seq, team_voc, h_devs = team_axes
    p = pl.program_id(0)
    kk = got_ref.shape[0] * CAP
    cols, width = o_ref.shape
    tiles = cols // LANES
    slice_rows = got_ref.shape[2] - LANES

    @pl.when(p == 0)
    def _():
        carry = got_ref[:, :, slice_rows:].reshape(kk, LANES)
        sel = lax.broadcasted_iota(jnp.int32, (16, LANES), 1) == HALF
        off = lax.dot_general(
            jnp.where(sel, 1.0, 0.0).astype(BF16),
            carry,
            (((1,), (1,)), ((), ())),
            preferred_element_type=F32,
        )[0:1]
        v = lax.broadcasted_iota(jnp.int32, (width, kk), 0).astype(F32)
        hot_ref[...] = jnp.where(off == v, 1.0, 0.0).astype(BF16)
        n = tot_ref.shape[0]
        k = lax.broadcasted_iota(jnp.int32, (n, kk), 1)
        member = k // CAP % team_seq * team_voc + k // (CAP * seq_devs * h_devs) % team_voc
        t = lax.broadcasted_iota(jnp.int32, (n, kk), 0)
        even = jnp.where(member == 2 * t, 1.0, 0.0).astype(BF16)
        odd = jnp.where(member == 2 * t + 1, 1.0, 0.0).astype(BF16)
        even = jnp.dot(even, carry, preferred_element_type=F32)
        odd = jnp.dot(odd, carry, preferred_element_type=F32)
        lane = lax.broadcasted_iota(jnp.int32, (n, LANES), 1)
        tot_ref[...] = jnp.where(lane < HALF, even, pltpu.roll(odd, HALF, 1))

    data = got_ref[:, :, pl.ds(pl.multiple_of(p * cols, LANES), cols)].reshape(kk, cols)
    counts = jnp.dot(hot_ref[...], data, preferred_element_type=F32)
    for i in range(tiles):
        pseudo = smooth_ref[pl.ds(p * tiles + i, 1), :] * ratio
        scale = VOCAB / (tot_ref[pl.ds(p * tiles + i, 1), :] + VOCAB * pseudo)
        done = (counts[:, i * LANES : (i + 1) * LANES] + pseudo) * scale
        o_ref[i * LANES : (i + 1) * LANES, :] = done.T


def shards(posteriors, token_block, token_offset, lengths, smoothing):
    rows, states = posteriors.shape
    seq_devs = lax.axis_size(SEQ)
    vocab_devs = lax.axis_size(VOC)
    devs = seq_devs * vocab_devs
    team = lax.axis_size(TEAM)
    width = VOCAB // vocab_devs
    slice_rows = states // seq_devs
    slots = vocab_devs * CAP
    chunk = slice_rows + LANES
    ratio = rows * devs / VOCAB
    params = pltpu.CompilerParams(vmem_limit_bytes=VMEM_LIMIT)
    smem = pl.BlockSpec(memory_space=pltpu.SMEM)
    steps = 2
    each = seq_devs // steps
    x_spec = pl.BlockSpec((rows, slice_rows * each), lambda s: (0, s))

    part = pl.pallas_call(
        functools.partial(part_kernel, rows, seq_devs, slice_rows),
        grid=(steps,),
        in_specs=[smem, x_spec],
        out_specs=pl.BlockSpec((team, seq_devs // 2, LANES), lambda s: (0, 0, 0)),
        out_shape=jax.ShapeDtypeStruct((team, seq_devs // 2, LANES), F32),
        scratch_shapes=[pltpu.VMEM((seq_devs, slice_rows), F32)],
        compiler_params=params,
        name="part",
    )(lengths, posteriors)
    sums = lax.all_to_all(part, TEAM, split_axis=0, concat_axis=0, tiled=True)

    row_spec = pl.BlockSpec((1, rows), lambda s: (0, 0))
    send = pl.pallas_call(
        functools.partial(bucket_kernel, rows, slots),
        grid=(steps,),
        in_specs=[smem, row_spec, row_spec, x_spec],
        out_specs=pl.BlockSpec((vocab_devs, each, CAP, chunk), lambda s: (0, s, 0, 0)),
        out_shape=jax.ShapeDtypeStruct((vocab_devs, seq_devs, CAP, chunk), BF16),
        scratch_shapes=[pltpu.VMEM((slots, rows), BF16)],
        compiler_params=params,
        cost_estimate=pl.CostEstimate(
            flops=2 * slots * rows * states, bytes_accessed=8 * rows * states, transcendentals=0
        ),
        name="bucket",
    )(lengths, token_block.reshape(1, rows), token_offset.reshape(1, rows), posteriors)

    tail = slice_rows // LANES
    send = pl.pallas_call(
        functools.partial(carry_kernel, seq_devs, slots),
        grid=(1,),
        in_specs=[
            pl.BlockSpec(memory_space=pltpu.VMEM),
            pl.BlockSpec((vocab_devs, 1, CAP, LANES), lambda i: (0, 0, 0, tail)),
        ],
        out_specs=pl.BlockSpec((vocab_devs, seq_devs, CAP, LANES), lambda i: (0, 0, 0, tail)),
        out_shape=jax.ShapeDtypeStruct((vocab_devs, seq_devs, CAP, chunk), BF16),
        input_output_aliases={1: 0},
        compiler_params=pltpu.CompilerParams(vmem_limit_bytes=52 * 2**20),
        name="carry",
    )(sums, send)

    send = send.reshape(devs, CAP, chunk)
    got = lax.all_to_all(send, VOC + SEQ, split_axis=0, concat_axis=0, tiled=True)

    cols = slice_rows // 2
    team_axes = (lax.axis_size(TEAM[:2]), lax.axis_size(TEAM[2:]), lax.axis_size(VOC[-1]))
    return pl.pallas_call(
        functools.partial(final_kernel, seq_devs, team_axes, ratio),
        grid=(slice_rows // cols,),
        in_specs=[
            pl.BlockSpec((tail, LANES), lambda p: (0, 0)),
            pl.BlockSpec(memory_space=pltpu.VMEM),
        ],
        out_specs=pl.BlockSpec((cols, width), lambda p: (p, 0)),
        out_shape=jax.ShapeDtypeStruct((slice_rows, width), F32),
        scratch_shapes=[
            pltpu.VMEM((width, devs * CAP), BF16),
            pltpu.VMEM((tail, LANES), F32),
        ],
        compiler_params=pltpu.CompilerParams(vmem_limit_bytes=32 * 2**20),
        name="final",
    )(smoothing.reshape(tail, LANES), got)


def solution(mesh):
    fine = Mesh(mesh.devices.reshape(2, 2, 2, 4, 2, 4, 2), SEQ + VOC)
    placed = (P(SEQ + VOC, None), P(SEQ + VOC, None), P(SEQ + VOC), P(), P(SEQ))
    return jax.shard_map(
        shards, mesh=fine, in_specs=placed, out_specs=P(SEQ, VOC), check_vma=False
    )
```

```python
import functools

import jax
import jax.numpy as jnp
from jax import lax
from jax.experimental import pallas as pl
from jax.experimental.pallas import tpu as pltpu
from jax.sharding import Mesh, PartitionSpec as P

VOCAB = 16384
SEQ = ("z1", "z0", "core")
VOC = ("yh", "yl", "x", "zhi")
TEAM = ("z0", "core", "yl", "x")
LANES = 128
CAP = 2
HALF = 64
F32 = jnp.float32
BF16 = jnp.bfloat16
VMEM_LIMIT = 60 * 2**20


def live_rows(rows, lengths_ref):
    bound = lengths_ref[lax.axis_index(SEQ)] - lax.axis_index(VOC) * rows
    return lambda shape, dim: lax.broadcasted_iota(jnp.int32, shape, dim) < bound


def part_kernel(rows, seq_devs, slice_rows, lengths_ref, x_ref, o_ref, acc_ref):
    p = pl.program_id(0)
    each = x_ref.shape[1] // slice_rows
    shape = (seq_devs, rows)
    live = live_rows(rows, lengths_ref)(shape, 1)
    total = jnp.zeros((seq_devs, slice_rows), F32)
    for i in range(each):
        mine = lax.broadcasted_iota(jnp.int32, shape, 0) == p * each + i
        left = jnp.where(live & mine, 1.0, 0.0).astype(BF16)
        block = x_ref[:, i * slice_rows : (i + 1) * slice_rows]
        total = total + jnp.dot(left, block, preferred_element_type=F32)

    @pl.when(p == 0)
    def _():
        acc_ref[...] = total

    @pl.when(p > 0)
    def _():
        acc_ref[...] += total

    @pl.when(p == pl.num_programs(0) - 1)
    def _():
        n = seq_devs // 2
        lane = lax.broadcasted_iota(jnp.int32, (n, LANES), 1)
        for t in range(slice_rows // LANES):
            tile = acc_ref[:, t * LANES : (t + 1) * LANES]
            turned = pltpu.roll(tile, HALF, 1)
            o_ref[2 * t] = jnp.where(lane < HALF, tile[:n], turned[n:])
            o_ref[2 * t + 1] = jnp.where(lane < HALF, turned[:n], tile[n:])


def bucket_kernel(rows, slots, lengths_ref, blk_ref, off_ref, x_ref, o_ref, pick_ref):
    n, each = o_ref.shape[:2]
    slice_rows = x_ref.shape[1] // each

    @pl.when(pl.program_id(0) == 0)
    def _():
        shape = (slots, rows)
        live = live_rows(rows, lengths_ref)(shape, 1)
        k = lax.broadcasted_iota(jnp.int32, shape, 0)
        hit = live & (blk_ref[...] == k // CAP)
        before = lax.broadcasted_iota(jnp.int32, (rows, rows), 0) < lax.broadcasted_iota(
            jnp.int32, (rows, rows), 1
        )
        rank = jnp.dot(
            jnp.where(hit, 1.0, 0.0).astype(BF16),
            jnp.where(before, 1.0, 0.0).astype(BF16),
            preferred_element_type=F32,
        )
        pick = hit & (rank == (k % CAP).astype(F32))
        pick_ref[...] = jnp.where(pick, 1.0, 0.0).astype(BF16)
        value = jnp.where(pick, (off_ref[...] + 1).astype(F32), 0.0)
        tag = jnp.sum(value, axis=1, keepdims=True) - 1.0
        lane = lax.broadcasted_iota(jnp.int32, (slots, LANES), 1)
        tag = jnp.where(lane == HALF, tag, 0.0).astype(BF16)
        o_ref[:, 0, :, slice_rows:] = tag.reshape(n, CAP, LANES)

    for i in range(each):
        block = x_ref[:, i * slice_rows : (i + 1) * slice_rows]
        y = jnp.dot(pick_ref[...], block, preferred_element_type=F32).astype(BF16)
        o_ref[:, i, :, :slice_rows] = y.reshape(n, CAP, slice_rows)


def carry_kernel(seq_devs, slots, sums_ref, tag_ref, o_ref):
    total = jnp.sum(sums_ref[...], axis=0)
    total = jnp.concatenate([total, pltpu.roll(total, HALF, 1)], axis=0)
    high = total.astype(BF16).astype(F32)
    low = total - high
    shape = (slots, LANES)
    odd = lax.broadcasted_iota(jnp.int32, shape, 0) % CAP == 1
    lane = lax.broadcasted_iota(jnp.int32, shape, 1)
    tag = tag_ref[...].reshape(slots, LANES).astype(F32)
    n = slots // CAP
    for s in range(seq_devs):
        both = jnp.where(odd, low[s : s + 1], high[s : s + 1])
        carry = jnp.where(lane < HALF, both, tag).astype(BF16)
        o_ref[:, s] = carry.reshape(n, CAP, LANES)


def final_kernel(seq_devs, team_axes, ratio, smooth_ref, got_ref, o_ref, hot_ref, tot_ref):
    team_seq, team_voc, h_devs = team_axes
    p = pl.program_id(0)
    kk = got_ref.shape[0] * CAP
    cols, width = o_ref.shape
    slice_rows = got_ref.shape[2] - LANES

    @pl.when(p == 0)
    def _():
        carry = got_ref[:, :, slice_rows:].reshape(kk, LANES)
        sel = lax.broadcasted_iota(jnp.int32, (16, LANES), 1) == HALF
        off = lax.dot_general(
            jnp.where(sel, 1.0, 0.0).astype(BF16),
            carry,
            (((1,), (1,)), ((), ())),
            preferred_element_type=F32,
        )[0:1]
        v = lax.broadcasted_iota(jnp.int32, (width, kk), 0).astype(F32)
        hot_ref[...] = jnp.where(off == v, 1.0, 0.0).astype(BF16)
        n = tot_ref.shape[0]
        k = lax.broadcasted_iota(jnp.int32, (n, kk), 1)
        member = k // CAP % team_seq * team_voc + k // (CAP * seq_devs * h_devs) % team_voc
        t = lax.broadcasted_iota(jnp.int32, (n, kk), 0)
        even = jnp.where(member == 2 * t, 1.0, 0.0).astype(BF16)
        odd = jnp.where(member == 2 * t + 1, 1.0, 0.0).astype(BF16)
        even = jnp.dot(even, carry, preferred_element_type=F32)
        odd = jnp.dot(odd, carry, preferred_element_type=F32)
        lane = lax.broadcasted_iota(jnp.int32, (n, LANES), 1)
        tot_ref[...] = jnp.where(lane < HALF, even, pltpu.roll(odd, HALF, 1))

    half = cols // 2
    for q in range(2):
        data = got_ref[:, :, q * half : (q + 1) * half].reshape(kk, half)
        counts = jnp.dot(hot_ref[...], data, preferred_element_type=F32)
        for i in range(half // LANES):
            t = q * (half // LANES) + i
            pseudo = smooth_ref[t : t + 1, :] * ratio
            scale = VOCAB / (tot_ref[t : t + 1, :] + VOCAB * pseudo)
            done = (counts[:, i * LANES : (i + 1) * LANES] + pseudo) * scale
            o_ref[t * LANES : (t + 1) * LANES, :] = done.T


def shards(posteriors, token_block, token_offset, lengths, smoothing):
    rows, states = posteriors.shape
    seq_devs = lax.axis_size(SEQ)
    vocab_devs = lax.axis_size(VOC)
    devs = seq_devs * vocab_devs
    team = lax.axis_size(TEAM)
    width = VOCAB // vocab_devs
    slice_rows = states // seq_devs
    slots = vocab_devs * CAP
    chunk = slice_rows + LANES
    ratio = rows * devs / VOCAB
    params = pltpu.CompilerParams(vmem_limit_bytes=VMEM_LIMIT)
    smem = pl.BlockSpec(memory_space=pltpu.SMEM)
    steps = 2
    each = seq_devs // steps
    x_spec = pl.BlockSpec((rows, slice_rows * each), lambda s: (0, s))

    part = pl.pallas_call(
        functools.partial(part_kernel, rows, seq_devs, slice_rows),
        grid=(steps,),
        in_specs=[smem, x_spec],
        out_specs=pl.BlockSpec((team, seq_devs // 2, LANES), lambda s: (0, 0, 0)),
        out_shape=jax.ShapeDtypeStruct((team, seq_devs // 2, LANES), F32),
        scratch_shapes=[pltpu.VMEM((seq_devs, slice_rows), F32)],
        compiler_params=params,
        name="part",
    )(lengths, posteriors)
    sums = lax.all_to_all(part, TEAM, split_axis=0, concat_axis=0, tiled=True)

    row_spec = pl.BlockSpec((1, rows), lambda s: (0, 0))
    send = pl.pallas_call(
        functools.partial(bucket_kernel, rows, slots),
        grid=(steps,),
        in_specs=[smem, row_spec, row_spec, x_spec],
        out_specs=pl.BlockSpec((vocab_devs, each, CAP, chunk), lambda s: (0, s, 0, 0)),
        out_shape=jax.ShapeDtypeStruct((vocab_devs, seq_devs, CAP, chunk), BF16),
        scratch_shapes=[pltpu.VMEM((slots, rows), BF16)],
        compiler_params=params,
        cost_estimate=pl.CostEstimate(
            flops=2 * slots * rows * states, bytes_accessed=8 * rows * states, transcendentals=0
        ),
        name="bucket",
    )(lengths, token_block.reshape(1, rows), token_offset.reshape(1, rows), posteriors)

    tail = slice_rows // LANES
    send = pl.pallas_call(
        functools.partial(carry_kernel, seq_devs, slots),
        grid=(1,),
        in_specs=[
            pl.BlockSpec(memory_space=pltpu.VMEM),
            pl.BlockSpec((vocab_devs, 1, CAP, LANES), lambda i: (0, 0, 0, tail)),
        ],
        out_specs=pl.BlockSpec((vocab_devs, seq_devs, CAP, LANES), lambda i: (0, 0, 0, tail)),
        out_shape=jax.ShapeDtypeStruct((vocab_devs, seq_devs, CAP, chunk), BF16),
        input_output_aliases={1: 0},
        compiler_params=pltpu.CompilerParams(vmem_limit_bytes=52 * 2**20),
        name="carry",
    )(sums, send)

    send = send.reshape(devs, CAP, chunk)
    got = lax.all_to_all(send, VOC + SEQ, split_axis=0, concat_axis=0, tiled=True)

    cols = slice_rows
    team_axes = (lax.axis_size(TEAM[:2]), lax.axis_size(TEAM[2:]), lax.axis_size(VOC[-1]))
    return pl.pallas_call(
        functools.partial(final_kernel, seq_devs, team_axes, ratio),
        grid=(slice_rows // cols,),
        in_specs=[
            pl.BlockSpec((tail, LANES), lambda p: (0, 0)),
            pl.BlockSpec(memory_space=pltpu.VMEM),
        ],
        out_specs=pl.BlockSpec((cols, width), lambda p: (p, 0)),
        out_shape=jax.ShapeDtypeStruct((slice_rows, width), F32),
        scratch_shapes=[
            pltpu.VMEM((width, devs * CAP), BF16),
            pltpu.VMEM((tail, LANES), F32),
        ],
        compiler_params=pltpu.CompilerParams(vmem_limit_bytes=32 * 2**20),
        name="final",
    )(smoothing.reshape(tail, LANES), got)


def solution(mesh):
    fine = Mesh(mesh.devices.reshape(2, 2, 2, 4, 2, 4, 2), SEQ + VOC)
    placed = (P(SEQ + VOC, None), P(SEQ + VOC, None), P(SEQ + VOC), P(), P(SEQ))
    return jax.shard_map(
        shards, mesh=fine, in_specs=placed, out_specs=P(SEQ, VOC), check_vma=False
    )
```

```python
import functools

import jax
import jax.numpy as jnp
from jax import lax
from jax.experimental import pallas as pl
from jax.experimental.pallas import tpu as pltpu
from jax.sharding import Mesh, PartitionSpec as P

VOCAB = 16384
SEQ = ("z1", "z0", "core")
VOC = ("yh", "yl", "x", "zhi")
TEAM = ("core", "z0", "yl", "x")
LANES = 128
CAP = 2
HALF = 64
F32 = jnp.float32
BF16 = jnp.bfloat16
VMEM_LIMIT = 60 * 2**20


def live_rows(rows, lengths_ref):
    bound = lengths_ref[lax.axis_index(SEQ)] - lax.axis_index(VOC) * rows
    return lambda shape, dim: lax.broadcasted_iota(jnp.int32, shape, dim) < bound


def part_kernel(rows, seq_devs, slice_rows, lengths_ref, x_ref, o_ref, acc_ref):
    p = pl.program_id(0)
    each = x_ref.shape[1] // slice_rows
    shape = (seq_devs, rows)
    live = live_rows(rows, lengths_ref)(shape, 1)
    total = jnp.zeros((seq_devs, slice_rows), F32)
    for i in range(each):
        mine = lax.broadcasted_iota(jnp.int32, shape, 0) == p * each + i
        left = jnp.where(live & mine, 1.0, 0.0).astype(BF16)
        block = x_ref[:, i * slice_rows : (i + 1) * slice_rows]
        total = total + jnp.dot(left, block, preferred_element_type=F32)

    @pl.when(p == 0)
    def _():
        acc_ref[...] = total

    @pl.when(p > 0)
    def _():
        acc_ref[...] += total

    @pl.when(p == pl.num_programs(0) - 1)
    def _():
        n = seq_devs // 2
        lane = lax.broadcasted_iota(jnp.int32, (n, LANES), 1)
        for t in range(slice_rows // LANES):
            tile = acc_ref[:, t * LANES : (t + 1) * LANES]
            turned = pltpu.roll(tile, HALF, 1)
            o_ref[2 * t] = jnp.where(lane < HALF, tile[:n], turned[n:])
            o_ref[2 * t + 1] = jnp.where(lane < HALF, turned[:n], tile[n:])


def bucket_kernel(rows, slots, lengths_ref, blk_ref, off_ref, x_ref, o_ref, pick_ref):
    n, each = o_ref.shape[:2]
    slice_rows = x_ref.shape[1] // each

    @pl.when(pl.program_id(0) == 0)
    def _():
        shape = (slots, rows)
        live = live_rows(rows, lengths_ref)(shape, 1)
        k = lax.broadcasted_iota(jnp.int32, shape, 0)
        hit = live & (blk_ref[...] == k // CAP)
        before = lax.broadcasted_iota(jnp.int32, (rows, rows), 0) < lax.broadcasted_iota(
            jnp.int32, (rows, rows), 1
        )
        rank = jnp.dot(
            jnp.where(hit, 1.0, 0.0).astype(BF16),
            jnp.where(before, 1.0, 0.0).astype(BF16),
            preferred_element_type=F32,
        )
        pick = hit & (rank == (k % CAP).astype(F32))
        pick_ref[...] = jnp.where(pick, 1.0, 0.0).astype(BF16)
        value = jnp.where(pick, (off_ref[...] + 1).astype(F32), 0.0)
        tag = jnp.sum(value, axis=1, keepdims=True) - 1.0
        lane = lax.broadcasted_iota(jnp.int32, (slots, LANES), 1)
        tag = jnp.where(lane == HALF, tag, 0.0).astype(BF16)
        o_ref[:, 0, :, slice_rows:] = tag.reshape(n, CAP, LANES)

    for i in range(each):
        block = x_ref[:, i * slice_rows : (i + 1) * slice_rows]
        y = jnp.dot(pick_ref[...], block, preferred_element_type=F32).astype(BF16)
        o_ref[:, i, :, :slice_rows] = y.reshape(n, CAP, slice_rows)


def carry_kernel(seq_devs, slots, sums_ref, tag_ref, o_ref):
    total = jnp.sum(sums_ref[...], axis=0)
    total = jnp.concatenate([total, pltpu.roll(total, HALF, 1)], axis=0)
    high = total.astype(BF16).astype(F32)
    low = total - high
    shape = (slots, LANES)
    odd = lax.broadcasted_iota(jnp.int32, shape, 0) % CAP == 1
    lane = lax.broadcasted_iota(jnp.int32, shape, 1)
    tag = tag_ref[...].reshape(slots, LANES).astype(F32)
    n = slots // CAP
    for s in range(seq_devs):
        both = jnp.where(odd, low[s : s + 1], high[s : s + 1])
        carry = jnp.where(lane < HALF, both, tag).astype(BF16)
        o_ref[:, s] = carry.reshape(n, CAP, LANES)


def final_kernel(seq_devs, team_axes, ratio, smooth_ref, got_ref, o_ref, hot_ref, tot_ref):
    team_seq, team_voc, h_devs = team_axes
    p = pl.program_id(0)
    kk = got_ref.shape[0] * CAP
    cols, width = o_ref.shape
    tiles = cols // LANES
    slice_rows = got_ref.shape[2] - LANES

    @pl.when(p == 0)
    def _():
        carry = got_ref[:, :, slice_rows:].reshape(kk, LANES)
        sel = lax.broadcasted_iota(jnp.int32, (16, LANES), 1) == HALF
        off = lax.dot_general(
            jnp.where(sel, 1.0, 0.0).astype(BF16),
            carry,
            (((1,), (1,)), ((), ())),
            preferred_element_type=F32,
        )[0:1]
        v = lax.broadcasted_iota(jnp.int32, (width, kk), 0).astype(F32)
        hot_ref[...] = jnp.where(off == v, 1.0, 0.0).astype(BF16)
        n = tot_ref.shape[0]
        k = lax.broadcasted_iota(jnp.int32, (n, kk), 1)
        pair = k // CAP % 2 * (team_seq // 2) + k // (CAP * 2) % (team_seq // 2)
        member = pair * team_voc + k // (CAP * seq_devs * h_devs) % team_voc
        t = lax.broadcasted_iota(jnp.int32, (n, kk), 0)
        even = jnp.where(member == 2 * t, 1.0, 0.0).astype(BF16)
        odd = jnp.where(member == 2 * t + 1, 1.0, 0.0).astype(BF16)
        even = jnp.dot(even, carry, preferred_element_type=F32)
        odd = jnp.dot(odd, carry, preferred_element_type=F32)
        lane = lax.broadcasted_iota(jnp.int32, (n, LANES), 1)
        tot_ref[...] = jnp.where(lane < HALF, even, pltpu.roll(odd, HALF, 1))

    data = got_ref[:, :, pl.ds(pl.multiple_of(p * cols, LANES), cols)].reshape(kk, cols)
    counts = jnp.dot(hot_ref[...], data, preferred_element_type=F32)
    for i in range(tiles):
        pseudo = smooth_ref[pl.ds(p * tiles + i, 1), :] * ratio
        scale = VOCAB / (tot_ref[pl.ds(p * tiles + i, 1), :] + VOCAB * pseudo)
        done = (counts[:, i * LANES : (i + 1) * LANES] + pseudo) * scale
        o_ref[i * LANES : (i + 1) * LANES, :] = done.T


def shards(posteriors, token_block, token_offset, lengths, smoothing):
    rows, states = posteriors.shape
    seq_devs = lax.axis_size(SEQ)
    vocab_devs = lax.axis_size(VOC)
    devs = seq_devs * vocab_devs
    team = lax.axis_size(TEAM)
    width = VOCAB // vocab_devs
    slice_rows = states // seq_devs
    slots = vocab_devs * CAP
    chunk = slice_rows + LANES
    ratio = rows * devs / VOCAB
    params = pltpu.CompilerParams(vmem_limit_bytes=VMEM_LIMIT)
    smem = pl.BlockSpec(memory_space=pltpu.SMEM)
    steps = 2
    each = seq_devs // steps
    x_spec = pl.BlockSpec((rows, slice_rows * each), lambda s: (0, s))

    part = pl.pallas_call(
        functools.partial(part_kernel, rows, seq_devs, slice_rows),
        grid=(steps,),
        in_specs=[smem, x_spec],
        out_specs=pl.BlockSpec((team, seq_devs // 2, LANES), lambda s: (0, 0, 0)),
        out_shape=jax.ShapeDtypeStruct((team, seq_devs // 2, LANES), F32),
        scratch_shapes=[pltpu.VMEM((seq_devs, slice_rows), F32)],
        compiler_params=params,
        name="part",
    )(lengths, posteriors)
    sums = lax.all_to_all(part, TEAM, split_axis=0, concat_axis=0, tiled=True)

    row_spec = pl.BlockSpec((1, rows), lambda s: (0, 0))
    send = pl.pallas_call(
        functools.partial(bucket_kernel, rows, slots),
        grid=(steps,),
        in_specs=[smem, row_spec, row_spec, x_spec],
        out_specs=pl.BlockSpec((vocab_devs, each, CAP, chunk), lambda s: (0, s, 0, 0)),
        out_shape=jax.ShapeDtypeStruct((vocab_devs, seq_devs, CAP, chunk), BF16),
        scratch_shapes=[pltpu.VMEM((slots, rows), BF16)],
        compiler_params=params,
        cost_estimate=pl.CostEstimate(
            flops=2 * slots * rows * states, bytes_accessed=8 * rows * states, transcendentals=0
        ),
        name="bucket",
    )(lengths, token_block.reshape(1, rows), token_offset.reshape(1, rows), posteriors)

    tail = slice_rows // LANES
    send = pl.pallas_call(
        functools.partial(carry_kernel, seq_devs, slots),
        grid=(1,),
        in_specs=[
            pl.BlockSpec(memory_space=pltpu.VMEM),
            pl.BlockSpec((vocab_devs, 1, CAP, LANES), lambda i: (0, 0, 0, tail)),
        ],
        out_specs=pl.BlockSpec((vocab_devs, seq_devs, CAP, LANES), lambda i: (0, 0, 0, tail)),
        out_shape=jax.ShapeDtypeStruct((vocab_devs, seq_devs, CAP, chunk), BF16),
        input_output_aliases={1: 0},
        compiler_params=pltpu.CompilerParams(vmem_limit_bytes=52 * 2**20),
        name="carry",
    )(sums, send)

    send = send.reshape(devs, CAP, chunk)
    got = lax.all_to_all(send, VOC + SEQ, split_axis=0, concat_axis=0, tiled=True)

    cols = slice_rows // 2
    team_axes = (lax.axis_size(TEAM[:2]), lax.axis_size(TEAM[2:]), lax.axis_size(VOC[-1]))
    return pl.pallas_call(
        functools.partial(final_kernel, seq_devs, team_axes, ratio),
        grid=(slice_rows // cols,),
        in_specs=[
            pl.BlockSpec((tail, LANES), lambda p: (0, 0)),
            pl.BlockSpec(memory_space=pltpu.VMEM),
        ],
        out_specs=pl.BlockSpec((cols, width), lambda p: (p, 0)),
        out_shape=jax.ShapeDtypeStruct((slice_rows, width), F32),
        scratch_shapes=[
            pltpu.VMEM((width, devs * CAP), BF16),
            pltpu.VMEM((tail, LANES), F32),
        ],
        compiler_params=pltpu.CompilerParams(vmem_limit_bytes=32 * 2**20),
        name="final",
    )(smoothing.reshape(tail, LANES), got)


def solution(mesh):
    fine = Mesh(mesh.devices.reshape(2, 2, 2, 4, 2, 4, 2), SEQ + VOC)
    placed = (P(SEQ + VOC, None), P(SEQ + VOC, None), P(SEQ + VOC), P(), P(SEQ))
    return jax.shard_map(
        shards, mesh=fine, in_specs=placed, out_specs=P(SEQ, VOC), check_vma=False
    )
```
